256 devices in a mesh: ka: 16 (over y, x_lo, core), ga: 16 (over x_hi, z).
Axes of the slice: x: 4 (x_hi: 2, x_lo: 2; x = x_hi * 2 + x_lo), y: 4, z: 8, core: 2. Of those that a mesh axis runs over, the one named last changes fastest.
Arguments:
- orbitals: bfloat16 [2, 16, 2, 16, 256], P(None, 'ka'), may hold values from -4 to 4
- fit_vectors: bfloat16 [2, 256, 12288], P(None, None, 'ga'), may hold values from -0.375 to 0.375
- screening: float32 [16, 2, 12288], P('ka', None, 'ga'), may hold values from 0.005 to 0.05
- qpoint_table: int32 [2, 2], replicated, may hold values from 0 to 1, as said below
Outputs:
- kernel: float32 [2, 3, 16, 128, 128], P(None, None, 'ka', 'ga')
The draws below stay inside these ranges and needn't reach their ends.
Inputs may be any that keep to these rules, and one draw needn't show every extreme that they name: qpoint_table[a, b] depends only on (a - b) mod 2.
All inputs are finite; a program needn't handle non-finite values.
Results may differ from the reference program's by a relative error of at most 0.0042.
Values may be sent and summed in bfloat16 or wider, within the bound.
No kernel may reach another device: no remote copies, remote signals or barrier semaphores. Data moves between devices by JAX's collectives and lax.ppermute only.
A program may use at most 64 MiB of HBM per device.

```python
import math
import jax
import jax.numpy as jnp
from jax import lax

NV = 8
NB = 16
NMU = 256
NG = 12288
NKY = 2
STEPS = 3
NKX = 16


def draw_qpoint_table(key, part):
    value_key = jax.random.fold_in(key, 11)
    place_key = jax.random.fold_in(key, 12)
    stored = jax.random.randint(value_key, (NKY,), 0, NKY).astype(jnp.int32)
    places_drawn = jax.random.permutation(place_key, NKY).astype(jnp.int32)
    stored = stored.at[places_drawn[0]].set(0)
    stored = stored.at[places_drawn[1]].set(NKY - 1)
    places = jnp.arange(NKY, dtype=jnp.int32)
    return stored[(places[:, None] - places[None, :]) % NKY].astype(jnp.int32)


def steps_of(key, shape, shards, low, top_value):
    gain = 1.0
    for axis_at, shards_of in shards:
        draws = jax.random.uniform(jax.random.fold_in(jax.random.fold_in(key, 6), axis_at), (shards_of,), jnp.float32, low / len(shards), top_value / len(shards))
        gain = gain * jnp.repeat(jnp.exp(draws), shape[axis_at] // shards_of).reshape((-1,) + (1,) * (len(shape) - 1 - axis_at))
    return gain


def bell_draw(stream_key, shape, scale, limit, pieces=(), kind=jnp.bfloat16):
    drawn = jax.random.normal(stream_key, shape, jnp.float32) * scale
    if len(pieces) > 0:
        drawn = steps_of(stream_key, shape, pieces, -0.22, 0.18) * drawn
    return jnp.clip(drawn, min=-limit, max=limit).astype(kind)


def setup_inputs(seed: int = 0) -> dict:
    key_list = jax.random.split(jax.random.key(seed), 5)
    return {
        "orbitals": bell_draw(key_list[0], (2, NKX, NKY, NB, NMU), 0.5, 4.0, ((1, 16),)),
        "fit_vectors": bell_draw(key_list[1], (2, NMU, NG), NMU ** -0.5, 0.375, ((2, 16),)),
        "screening": jnp.clip(jnp.exp(math.log(0.05) - 2.3025851 * jax.random.uniform(key_list[2], (NKX, NKY, NG), jnp.float32) ** steps_of(key_list[2], (NKX, NKY, NG), ((0, 16), (2, 16)), -0.2, 0.2)), 0.005, 0.05),
        "qpoint_table": draw_qpoint_table(jax.random.fold_in(key_list[4], 71), 0),
    }


def densities(first_band, second_band, fit_vectors):
    points = first_band.shape[-1]
    first_real = first_band[0].astype(jnp.float32)[:, :, None, None, :]
    first_imag = first_band[1].astype(jnp.float32)[:, :, None, None, :]
    second_real = second_band[0].astype(jnp.float32)[None, None, :, :, :]
    second_imag = second_band[1].astype(jnp.float32)[None, None, :, :, :]
    pair_real = (first_real * second_real + first_imag * second_imag).astype(jnp.bfloat16).reshape(-1, points)
    pair_imag = (first_real * second_imag - first_imag * second_real).astype(jnp.bfloat16).reshape(-1, points)
    density_real = jnp.dot(pair_real, fit_vectors[0], preferred_element_type=jnp.float32) - jnp.dot(pair_imag, fit_vectors[1], preferred_element_type=jnp.float32)
    density_imag = jnp.dot(pair_real, fit_vectors[1], preferred_element_type=jnp.float32) + jnp.dot(pair_imag, fit_vectors[0], preferred_element_type=jnp.float32)
    return density_real.astype(jnp.bfloat16), density_imag.astype(jnp.bfloat16)


def mixing(first, second):
    return jnp.einsum("abdeg,ahdig->abhdei", first.astype(jnp.float32), second.astype(jnp.float32))


def kernel_block(home_orbitals, far_orbitals, fit_vectors, pair_screen):
    kys = home_orbitals.shape[1]
    valence = NV
    conduct = home_orbitals.shape[2] - valence
    width = fit_vectors.shape[2]
    cond_real, cond_imag = densities(home_orbitals[:, :, valence:], far_orbitals[:, :, valence:], fit_vectors)
    val_real, val_imag = densities(home_orbitals[:, :, :valence], far_orbitals[:, :, :valence], fit_vectors)
    cond_real = cond_real.reshape(kys, conduct, kys, conduct, width)
    cond_imag = cond_imag.reshape(kys, conduct, kys, conduct, width)
    screen_wide = pair_screen[:, None, :, None, :]
    weight_real = (val_real.reshape(kys, valence, kys, valence, width).astype(jnp.float32) * screen_wide).astype(jnp.bfloat16)
    weight_imag = (val_imag.reshape(kys, valence, kys, valence, width).astype(jnp.float32) * screen_wide).astype(jnp.bfloat16)
    kernel_real = mixing(cond_real, weight_real) + mixing(cond_imag, weight_imag)
    kernel_imag = mixing(cond_real, weight_imag) - mixing(cond_imag, weight_real)
    row_count = kys * conduct * valence
    return jnp.stack([kernel_real.reshape(row_count, row_count), kernel_imag.reshape(row_count, row_count)], 0)


def reference(orbitals, fit_vectors, screening, qpoint_table):
    by_row = jnp.moveaxis(orbitals, 1, 0)
    outputs = []
    for distance in range(1, STEPS + 1):
        far_rows = jnp.roll(by_row, distance, axis=0)
        pair_screen = jnp.take(screening[distance], qpoint_table, axis=0)
        blocks = lax.map(lambda rows_pair: kernel_block(rows_pair[0], rows_pair[1], fit_vectors, pair_screen), (by_row, far_rows))
        outputs.append(jnp.moveaxis(blocks, 0, 1))
    return jnp.stack(outputs, 1)
```

```python
import jax
import jax.numpy as jnp
from jax import lax
from jax.experimental import pallas as pl
from jax.experimental.pallas import tpu as pltpu
from jax.sharding import PartitionSpec as P

NV = 8
STEPS = 3
BF16 = jnp.bfloat16
F32 = jnp.float32
VMEM_LIMIT = 24 * 1024 * 1024


def call(kernel, out_shapes, operands, spaces, scratch=(), flops=0, moved=0):
    specs = [pl.BlockSpec(memory_space=space) for space in spaces]
    out_specs = [pl.BlockSpec(memory_space=pltpu.VMEM) for _ in out_shapes]
    return pl.pallas_call(
        kernel,
        out_shape=[jax.ShapeDtypeStruct(shape, kind) for shape, kind in out_shapes],
        in_specs=specs,
        out_specs=out_specs,
        scratch_shapes=list(scratch),
        compiler_params=pltpu.CompilerParams(vmem_limit_bytes=VMEM_LIMIT),
        cost_estimate=pl.CostEstimate(flops=flops, bytes_accessed=moved, transcendentals=0),
    )(*operands)


def payload_kernel(orbital_ref, screen_ref, out_ref):
    out_ref[0:64, :] = orbital_ref[...]
    pieces = []
    for q in range(2):
        for j in range(3):
            pieces.append(screen_ref[q : q + 1, 256 * j : 256 * (j + 1)])
    rows = jnp.concatenate(pieces + [jnp.zeros((2, 256), F32)], axis=0)
    high = rows.astype(BF16)
    low = (rows - high.astype(F32)).astype(BF16)
    out_ref[64:80, :] = jnp.concatenate([high.astype(F32), low.astype(F32)], axis=0).astype(BF16)


def density_kernel(home_ref, far1_ref, far2_ref, far3_ref, fit_ref, cond_ref, val_ref, pair_ref):
    width = fit_ref.shape[1]
    for kind, out_ref in ((1, cond_ref), (0, val_ref)):
        for step, far_ref in enumerate((far1_ref, far2_ref, far3_ref)):
            for a in range(2):
                top = a * 16 + kind * 8
                home_r = home_ref[top : top + 8, :].astype(F32)[:, None, :]
                home_i = home_ref[32 + top : 40 + top, :].astype(F32)[:, None, :]
                for b in range(2):
                    top = b * 16 + kind * 8
                    far_r = far_ref[top : top + 8, :].astype(F32)[None]
                    far_i = far_ref[32 + top : 40 + top, :].astype(F32)[None]
                    real = (home_r * far_r + home_i * far_i).reshape(64, 256).astype(BF16)
                    imag = (home_r * far_i - home_i * far_r).reshape(64, 256).astype(BF16)
                    at = (a * 2 + b) * 64
                    pair_ref[at : at + 64, 0:256] = real
                    pair_ref[at : at + 64, 256:512] = -imag
                    pair_ref[256 + at : 320 + at, 0:256] = imag
                    pair_ref[256 + at : 320 + at, 256:512] = real
            for part in range(2):
                out_ref[step, :, part * width : (part + 1) * width] = jnp.dot(
                    pair_ref[part * 256 : (part + 1) * 256, :], fit_ref[...], preferred_element_type=F32
                ).astype(BF16)


def mixing_kernel(
    table_ref, cond_ref, val_ref, win0_ref, win1_ref, win2_ref, win3_ref, own_ref, out1_ref, out2_ref, out3_ref,
    weight_ref, all_ref,
):
    width = cond_ref.shape[2] // 2
    row = lax.axis_index("ka")
    for step in range(STEPS):
        away = lax.rem(row - (step + 1) + 16, 16)
        hop, slot = away // 4, lax.rem(away, 4)
        found = [ref[slot].astype(F32) for ref in (win0_ref, win1_ref, win2_ref, win3_ref)]
        rows = jnp.where(hop == 0, found[0], jnp.where(hop == 1, found[1], jnp.where(hop == 2, found[2], found[3])))
        rows = rows[0:8] + rows[8:16]
        stored = [
            jnp.concatenate([rows[3 * q + j : 3 * q + j + 1] for j in range(3)], axis=1) for q in range(2)
        ]
        for a in range(2):
            blocks = []
            for b in range(2):
                screen = jnp.where(table_ref[a, b] == 0, stored[0], stored[1])
                at = (a * 2 + b) * 64
                val_r = val_ref[step, at : at + 64, 0:width].astype(F32)
                val_i = val_ref[step, at : at + 64, width:].astype(F32)
                weight_r = (val_r * screen).astype(BF16)
                weight_i = (val_i * screen).astype(BF16)
                weight_ref[0:64, 0:width] = weight_r
                weight_ref[0:64, width:] = weight_i
                weight_ref[64:128, 0:width] = weight_i
                weight_ref[64:128, width:] = -weight_r
                block = lax.dot_general(
                    cond_ref[step, at : at + 64, :], weight_ref[...], (((1,), (1,)), ((), ())),
                    preferred_element_type=F32,
                )
                blocks.append(block.reshape(8, 8, 128))
            both = jnp.concatenate(blocks, axis=1).astype(BF16)
            for c in range(8):
                all_ref[a * 2 + c % 2, c // 2, step * 16 : (step + 1) * 16, :] = both[c]
    place = lax.axis_index("ga")
    mine = (place // 8) * 2 + lax.rem(place, 2)
    for m, out_ref in enumerate((own_ref, out1_ref, out2_ref, out3_ref)):
        out_ref[...] = all_ref[mine ^ m]


def middle_kernel(own_ref, in1_ref, in2_ref, in3_ref, keep_ref, out1_ref, out2_ref, out3_ref):
    mine = lax.rem(lax.axis_index("ga"), 8) // 2
    for m, out_ref in enumerate((keep_ref, out1_ref, out2_ref, out3_ref)):
        total = own_ref[mine ^ m].astype(F32)
        for ref in (in1_ref, in2_ref, in3_ref):
            total = total + ref[mine ^ m].astype(F32)
        out_ref[...] = total


def final_kernel(own_ref, in1_ref, in2_ref, in3_ref, out_ref):
    sublane = lax.broadcasted_iota(jnp.int32, (8, 128), 0)
    lane = lax.broadcasted_iota(jnp.int32, (8, 128), 1) // 8
    for step in range(STEPS):
        sides = []
        for b in range(2):
            at = (step * 2 + b) * 8
            x = own_ref[at : at + 8, :]
            for ref in (in1_ref, in2_ref, in3_ref):
                x = x + ref[at : at + 8, :]
            for k in range(3):
                bit = 1 << k
                low = (sublane & bit) == 0
                low_lane = (lane & bit) == 0
                from_below = pltpu.roll(pltpu.roll(x, 8 - bit, 0), 8 * bit, 1)
                from_above = pltpu.roll(pltpu.roll(x, bit, 0), 128 - 8 * bit, 1)
                x = jnp.where(low == low_lane, x, jnp.where(low, from_below, from_above))
            sides.append(x)
        first_half = lane < 8
        out_ref[0, step] = jnp.where(first_half, sides[0], pltpu.roll(sides[1], 64, 1))
        out_ref[1, step] = jnp.where(first_half, pltpu.roll(sides[0], 64, 1), sides[1])


def body(orbitals, fit_vectors, screening, qpoint_table):
    vmem, smem = pltpu.VMEM, pltpu.SMEM
    width = fit_vectors.shape[2]
    rows = 16

    def shifted(x, by, sources=range(16)):
        return lax.ppermute(x, "ka", [(i, (i + by) % rows) for i in sources])

    def swapped(x, mask):
        return lax.ppermute(x, "ga", [(i, i ^ mask) for i in range(16)])

    (home,) = call(
        payload_kernel, [((80, 256), BF16)], (orbitals.reshape(64, 256), screening[0]), (vmem, vmem)
    )
    far = [shifted(home, by) for by in (1, 2, 3)]
    window = jnp.stack([x[64:80] for x in [home] + far])
    windows = [shifted(window, by, range(1, 7)) for by in (4, 8, 12)]
    cond, val = call(
        density_kernel,
        [((STEPS, 256, 2 * width), BF16)] * 2,
        (home, *far, fit_vectors.reshape(512, width)),
        (vmem,) * 5,
        [pltpu.VMEM((512, 512), BF16)],
        flops=2 * STEPS * 8 * 256 * 256 * width,
        moved=6_000_000,
    )
    parts = call(
        mixing_kernel,
        [((4, 48, 128), BF16)] * 4,
        (qpoint_table, cond, val, window, *windows),
        (smem,) + (vmem,) * 6,
        [pltpu.VMEM((128, 2 * width), BF16), pltpu.VMEM((4, 4, 48, 128), BF16)],
        flops=2 * STEPS * 4 * 4 * 64 * 64 * width,
        moved=6_000_000,
    )
    received = [swapped(x, mask) for x, mask in zip(parts[1:], (1, 8, 9))]
    sums = call(middle_kernel, [((48, 128), F32)] * 4, (parts[0], *received), (vmem,) * 4)
    received = [swapped(x, mask) for x, mask in zip(sums[1:], (2, 4, 6))]
    (out,) = call(final_kernel, [((2, STEPS, 8, 128), F32)], (sums[0], *received), (vmem,) * 4)
    return out[:, :, None]


def solution(mesh):
    in_specs = (P(None, "ka", None, None, None), P(None, None, "ga"), P("ka", None, "ga"), P())
    out_specs = P(None, None, "ka", "ga", None)
    return jax.shard_map(body, mesh=mesh, in_specs=in_specs, out_specs=out_specs, check_vma=False)
```

```python
import jax
import jax.numpy as jnp
from jax import lax
from jax.experimental import pallas as pl
from jax.experimental.pallas import tpu as pltpu
from jax.sharding import PartitionSpec as P

NV = 8
STEPS = 3
BF16 = jnp.bfloat16
F32 = jnp.float32
VMEM_LIMIT = 10 * 1024 * 1024


def call(kernel, out_shapes, operands, spaces, scratch=(), flops=0, moved=0):
    specs = [pl.BlockSpec(memory_space=space) for space in spaces]
    out_specs = [pl.BlockSpec(memory_space=pltpu.VMEM) for _ in out_shapes]
    return pl.pallas_call(
        kernel,
        out_shape=[jax.ShapeDtypeStruct(shape, kind) for shape, kind in out_shapes],
        in_specs=specs,
        out_specs=out_specs,
        scratch_shapes=list(scratch),
        compiler_params=pltpu.CompilerParams(vmem_limit_bytes=VMEM_LIMIT),
        cost_estimate=pl.CostEstimate(flops=flops, bytes_accessed=moved, transcendentals=0),
    )(*operands)


def payload_kernel(screen_ref, out_ref):
    pieces = []
    for q in range(2):
        for j in range(3):
            pieces.append(screen_ref[q : q + 1, 256 * j : 256 * (j + 1)])
    rows = jnp.concatenate(pieces + [jnp.zeros((2, 256), F32)], axis=0)
    high = rows.astype(BF16)
    low = (rows - high.astype(F32)).astype(BF16)
    block = jnp.concatenate([high.astype(F32), low.astype(F32)], axis=0).astype(BF16)
    for target in range(16):
        out_ref[target] = block


def fetch_kernel(fit_ref, home_ref, fit_out_ref, home_out_ref, sem):
    first = pltpu.make_async_copy(fit_ref, fit_out_ref, sem.at[0])
    second = pltpu.make_async_copy(home_ref, home_out_ref, sem.at[1])
    first.start()
    second.start()
    first.wait()
    second.wait()


def density_kernel(home_ref, far1_ref, far2_ref, far3_ref, fit_ref, out_ref, pair_ref):
    width = fit_ref.shape[1]
    for kind in range(2):
        for step, far_ref in enumerate((far1_ref, far2_ref, far3_ref)):
            for a in range(2):
                top = a * 16 + kind * 8
                home_r = home_ref[top : top + 8, :].astype(F32)[:, None, :]
                home_i = home_ref[32 + top : 40 + top, :].astype(F32)[:, None, :]
                for b in range(2):
                    top = b * 16 + kind * 8
                    far_r = far_ref[top : top + 8, :].astype(F32)[None]
                    far_i = far_ref[32 + top : 40 + top, :].astype(F32)[None]
                    real = (home_r * far_r + home_i * far_i).reshape(64, 256).astype(BF16)
                    imag = (home_r * far_i - home_i * far_r).reshape(64, 256).astype(BF16)
                    at = (a * 2 + b) * 64
                    pair_ref[at : at + 64, 0:256] = real
                    pair_ref[at : at + 64, 256:512] = -imag
                    pair_ref[256 + at : 320 + at, 0:256] = imag
                    pair_ref[256 + at : 320 + at, 256:512] = real
            for part in range(2):
                out_ref[kind, step, :, part * width : (part + 1) * width] = jnp.dot(
                    pair_ref[part * 256 : (part + 1) * 256, :], fit_ref[...], preferred_element_type=F32
                ).astype(BF16)


def mixing_kernel(table_ref, density_ref, screen_ref, out_ref, weight_ref):
    width = density_ref.shape[3] // 2
    for step in range(STEPS):
        rows = screen_ref[step + 1].astype(F32)
        rows = rows[0:8] + rows[8:16]
        stored = [
            jnp.concatenate([rows[3 * q + j : 3 * q + j + 1] for j in range(3)], axis=1) for q in range(2)
        ]
        for a in range(2):
            blocks = []
            for b in range(2):
                screen = jnp.where(table_ref[a, b] == 0, stored[0], stored[1])
                at = (a * 2 + b) * 64
                val_r = density_ref[0, step, at : at + 64, 0:width].astype(F32)
                val_i = density_ref[0, step, at : at + 64, width:].astype(F32)
                weight_r = (val_r * screen).astype(BF16)
                weight_i = (val_i * screen).astype(BF16)
                weight_ref[0:64, 0:width] = weight_r
                weight_ref[0:64, width:] = weight_i
                weight_ref[64:128, 0:width] = weight_i
                weight_ref[64:128, width:] = -weight_r
                block = lax.dot_general(
                    density_ref[1, step, at : at + 64, :], weight_ref[...], (((1,), (1,)), ((), ())),
                    preferred_element_type=F32,
                )
                blocks.append(block.reshape(8, 8, 128))
            both = jnp.concatenate(blocks, axis=1).astype(BF16)
            for c in range(8):
                out_ref[a * 8 + c, step * 16 : (step + 1) * 16, :] = both[c]


def final_kernel(in_ref, out_ref):
    sublane = lax.broadcasted_iota(jnp.int32, (8, 128), 0)
    lane = lax.broadcasted_iota(jnp.int32, (8, 128), 1) // 8
    for step in range(STEPS):
        total = in_ref[0, step * 16 : (step + 1) * 16, :].astype(F32)
        for source in range(1, 16):
            total = total + in_ref[source, step * 16 : (step + 1) * 16, :].astype(F32)
        sides = []
        for b in range(2):
            x = total[b * 8 : (b + 1) * 8]
            for k in range(3):
                bit = 1 << k
                low = (sublane & bit) == 0
                low_lane = (lane & bit) == 0
                from_below = pltpu.roll(pltpu.roll(x, 8 - bit, 0), 8 * bit, 1)
                from_above = pltpu.roll(pltpu.roll(x, bit, 0), 128 - 8 * bit, 1)
                x = jnp.where(low == low_lane, x, jnp.where(low, from_below, from_above))
            sides.append(x)
        first_half = lane < 8
        out_ref[0, step] = jnp.where(first_half, sides[0], pltpu.roll(sides[1], 64, 1))
        out_ref[1, step] = jnp.where(first_half, pltpu.roll(sides[0], 64, 1), sides[1])


def body(orbitals, fit_vectors, screening, qpoint_table):
    vmem, smem = pltpu.VMEM, pltpu.SMEM
    width = fit_vectors.shape[2]
    home = orbitals.reshape(64, 256)
    far = [
        lax.ppermute(home, "ka", [(i, (i + by) % 16) for i in range(16)]) for by in range(1, STEPS + 1)
    ]
    (payload,) = call(payload_kernel, [((16, 16, 256), BF16)], (screening[0],), (vmem,), moved=200_000)
    screens = lax.all_to_all(payload, "ka", 0, 0)
    fit, home = call(
        fetch_kernel, [((512, width), BF16), ((64, 256), BF16)], (fit_vectors.reshape(512, width), home),
        (pltpu.HBM,) * 2, [pltpu.SemaphoreType.DMA((2,))], moved=1_600_000,
    )
    (density,) = call(
        density_kernel,
        [((2, STEPS, 256, 2 * width), BF16)],
        (home, *far, fit),
        (vmem,) * 5,
        [pltpu.VMEM((512, 512), BF16)],
        flops=2 * STEPS * 8 * 256 * 256 * width,
        moved=6_000_000,
    )
    (parts,) = call(
        mixing_kernel,
        [((16, 48, 128), BF16)],
        (qpoint_table, density, screens),
        (smem,) + (vmem,) * 2,
        [pltpu.VMEM((128, 2 * width), BF16)],
        flops=2 * STEPS * 4 * 4 * 64 * 64 * width,
        moved=6_000_000,
    )
    parts = lax.all_to_all(parts, "ga", 0, 0)
    (out,) = call(final_kernel, [((2, STEPS, 8, 128), F32)], (parts,), (vmem,))
    return out[:, :, None]


def solution(mesh):
    in_specs = (P(None, "ka", None, None, None), P(None, None, "ga"), P("ka", None, "ga"), P())
    out_specs = P(None, None, "ka", "ga", None)
    return jax.shard_map(body, mesh=mesh, in_specs=in_specs, out_specs=out_specs, check_vma=False)
```

```python
import jax
import jax.numpy as jnp
from jax import lax
from jax.experimental import pallas as pl
from jax.experimental.pallas import tpu as pltpu
from jax.sharding import PartitionSpec as P

NV = 8
STEPS = 3
BF16 = jnp.bfloat16
F32 = jnp.float32
VMEM_LIMIT = 10 * 1024 * 1024


def call(kernel, out_shapes, operands, spaces, scratch=(), flops=0, moved=0):
    specs = [pl.BlockSpec(memory_space=space) for space in spaces]
    out_specs = [pl.BlockSpec(memory_space=pltpu.VMEM) for _ in out_shapes]
    return pl.pallas_call(
        kernel,
        out_shape=[jax.ShapeDtypeStruct(shape, kind) for shape, kind in out_shapes],
        in_specs=specs,
        out_specs=out_specs,
        scratch_shapes=list(scratch),
        compiler_params=pltpu.CompilerParams(vmem_limit_bytes=VMEM_LIMIT),
        cost_estimate=pl.CostEstimate(flops=flops, bytes_accessed=moved, transcendentals=0),
    )(*operands)


def payload_kernel(orbital_ref, own_ref, in1_ref, in2_ref, in3_ref, out_ref):
    out_ref[0:64, :] = orbital_ref[...]
    screen = jnp.where(lax.axis_index("ka") < 4, own_ref[...], in1_ref[...] + in2_ref[...] + in3_ref[...])
    pieces = []
    for q in range(2):
        for j in range(3):
            pieces.append(screen[q : q + 1, 256 * j : 256 * (j + 1)])
    rows = jnp.concatenate(pieces + [jnp.zeros((2, 256), F32)], axis=0)
    high = rows.astype(BF16)
    low = (rows - high.astype(F32)).astype(BF16)
    out_ref[64:80, :] = jnp.concatenate([high.astype(F32), low.astype(F32)], axis=0).astype(BF16)


def fetch_kernel(*refs):
    count = len(refs) // 2
    copies = [pltpu.make_async_copy(refs[i], refs[count + i], refs[-1].at[i]) for i in range(count)]
    for copy in copies:
        copy.start()
    for copy in copies:
        copy.wait()


def density_kernel(home_ref, far_ref, fit_ref, out_ref, pair_ref):
    width = fit_ref.shape[1]
    for kind in range(2):
        for a in range(2):
            top = a * 16 + kind * 8
            home_r = home_ref[top : top + 8, :].astype(F32)[:, None, :]
            home_i = home_ref[32 + top : 40 + top, :].astype(F32)[:, None, :]
            for b in range(2):
                top = b * 16 + kind * 8
                far_r = far_ref[top : top + 8, :].astype(F32)[None]
                far_i = far_ref[32 + top : 40 + top, :].astype(F32)[None]
                real = (home_r * far_r + home_i * far_i).reshape(64, 256).astype(BF16)
                imag = (home_r * far_i - home_i * far_r).reshape(64, 256).astype(BF16)
                at = (a * 2 + b) * 64
                pair_ref[at : at + 64, 0:256] = real
                pair_ref[at : at + 64, 256:512] = -imag
                pair_ref[256 + at : 320 + at, 0:256] = imag
                pair_ref[256 + at : 320 + at, 256:512] = real
        for part in range(2):
            out_ref[kind, :, part * width : (part + 1) * width] = jnp.dot(
                pair_ref[part * 256 : (part + 1) * 256, :], fit_ref[...], preferred_element_type=F32
            ).astype(BF16)


def mixing_kernel(
    table_ref, home_ref, far1_ref, far2_ref, far3_ref, fit_ref, density1_ref, density2_ref, out_ref,
    density3_ref, pair_ref, weight_ref,
):
    density_kernel(home_ref, far3_ref, fit_ref, density3_ref, pair_ref)
    width = fit_ref.shape[1]
    place = lax.rem(lax.axis_index("ka"), 4)
    sent = [ref[64:80, :].astype(F32) for ref in (home_ref, far1_ref, far2_ref, far3_ref)]
    sent = [x[0:8] + x[8:16] for x in sent]
    for step, density_ref in enumerate((density1_ref, density2_ref, density3_ref)):
        away = lax.rem(place - (step + 1) + 4, 4)
        rows = jnp.where(away == 0, sent[0], jnp.where(away == 1, sent[1], jnp.where(away == 2, sent[2], sent[3])))
        stored = [
            jnp.concatenate([rows[3 * q + j : 3 * q + j + 1] for j in range(3)], axis=1) for q in range(2)
        ]
        for a in range(2):
            blocks = []
            for b in range(2):
                screen = jnp.where(table_ref[a, b] == 0, stored[0], stored[1])
                at = (a * 2 + b) * 64
                val_r = density_ref[0, at : at + 64, 0:width].astype(F32)
                val_i = density_ref[0, at : at + 64, width:].astype(F32)
                weight_r = (val_r * screen).astype(BF16)
                weight_i = (val_i * screen).astype(BF16)
                weight_ref[0:64, 0:width] = weight_r
                weight_ref[0:64, width:] = weight_i
                weight_ref[64:128, 0:width] = weight_i
                weight_ref[64:128, width:] = -weight_r
                block = lax.dot_general(
                    density_ref[1, at : at + 64, :], weight_ref[...], (((1,), (1,)), ((), ())),
                    preferred_element_type=F32,
                )
                blocks.append(block.reshape(8, 8, 128))
            both = jnp.concatenate(blocks, axis=1).astype(BF16)
            for c in range(8):
                out_ref[a * 8 + c, step * 16 : (step + 1) * 16, :] = both[c]


def final_kernel(in_ref, out_ref):
    sublane = lax.broadcasted_iota(jnp.int32, (8, 128), 0)
    lane = lax.broadcasted_iota(jnp.int32, (8, 128), 1) // 8
    for step in range(STEPS):
        total = in_ref[0, step * 16 : (step + 1) * 16, :].astype(F32)
        for source in range(1, 16):
            total = total + in_ref[source, step * 16 : (step + 1) * 16, :].astype(F32)
        sides = []
        for b in range(2):
            x = total[b * 8 : (b + 1) * 8]
            for k in range(3):
                bit = 1 << k
                low = (sublane & bit) == 0
                low_lane = (lane & bit) == 0
                from_below = pltpu.roll(pltpu.roll(x, 8 - bit, 0), 8 * bit, 1)
                from_above = pltpu.roll(pltpu.roll(x, bit, 0), 128 - 8 * bit, 1)
                x = jnp.where(low == low_lane, x, jnp.where(low, from_below, from_above))
            sides.append(x)
        first_half = lane < 8
        out_ref[0, step] = jnp.where(first_half, sides[0], pltpu.roll(sides[1], 64, 1))
        out_ref[1, step] = jnp.where(first_half, pltpu.roll(sides[0], 64, 1), sides[1])


def body(orbitals, fit_vectors, screening, qpoint_table):
    vmem, smem = pltpu.VMEM, pltpu.SMEM
    width = fit_vectors.shape[2]

    def shifted(x, by, sources=range(16)):
        return lax.ppermute(x, "ka", [(i, (i + by) % 16) for i in sources])

    screen = screening[0]
    screens = [shifted(screen, by, range(1, STEPS + 1)) for by in (4, 8, 12)]
    given = (fit_vectors.reshape(512, width), orbitals.reshape(64, 256), screen)
    fit, own, own_screen = call(
        fetch_kernel, [(x.shape, x.dtype) for x in given],
        [pltpu.with_memory_space_constraint(x, pltpu.HBM) for x in given],
        (pltpu.HBM,) * 3, [pltpu.SemaphoreType.DMA((3,))], moved=1_700_000,
    )
    (home,) = call(payload_kernel, [((80, 256), BF16)], (own, own_screen, *screens), (vmem,) * 5)
    far = [shifted(home, by) for by in range(1, STEPS + 1)]
    pairs = pltpu.VMEM((512, 512), BF16)
    densities = [
        call(
            density_kernel, [((2, 256, 2 * width), BF16)], (home, x, fit), (vmem,) * 3, [pairs],
            flops=2 * 8 * 256 * 256 * width, moved=2_000_000,
        )[0]
        for x in far[:2]
    ]
    (parts,) = call(
        mixing_kernel,
        [((16, 48, 128), BF16)],
        (qpoint_table, home, *far, fit, *densities),
        (smem,) + (vmem,) * 7,
        [pltpu.VMEM((2, 256, 2 * width), BF16), pairs, pltpu.VMEM((128, 2 * width), BF16)],
        flops=2 * (STEPS * 4 * 4 * 64 * 64 + 8 * 256 * 256) * width,
        moved=6_000_000,
    )
    parts = lax.all_to_all(parts, "ga", 0, 0)
    (out,) = call(final_kernel, [((2, STEPS, 8, 128), F32)], (parts,), (vmem,))
    return out[:, :, None]


def solution(mesh):
    in_specs = (P(None, "ka", None, None, None), P(None, None, "ga"), P("ka", None, "ga"), P())
    out_specs = P(None, None, "ka", "ga", None)
    return jax.shard_map(body, mesh=mesh, in_specs=in_specs, out_specs=out_specs, check_vma=False)
```

```python
import jax
import jax.numpy as jnp
from jax import lax
from jax.experimental import pallas as pl
from jax.experimental.pallas import tpu as pltpu
from jax.sharding import PartitionSpec as P

NV = 8
STEPS = 3
BF16 = jnp.bfloat16
F32 = jnp.float32
VMEM_LIMIT = 10 * 1024 * 1024


def call(kernel, out_shapes, operands, spaces, scratch=(), flops=0, moved=0):
    specs = [pl.BlockSpec(memory_space=space) for space in spaces]
    out_specs = [pl.BlockSpec(memory_space=pltpu.VMEM) for _ in out_shapes]
    return pl.pallas_call(
        kernel,
        out_shape=[jax.ShapeDtypeStruct(shape, kind) for shape, kind in out_shapes],
        in_specs=specs,
        out_specs=out_specs,
        scratch_shapes=list(scratch),
        compiler_params=pltpu.CompilerParams(vmem_limit_bytes=VMEM_LIMIT),
        cost_estimate=pl.CostEstimate(flops=flops, bytes_accessed=moved, transcendentals=0),
    )(*operands)


def row_kernel(own_ref, in1_ref, in2_ref, in3_ref, out_ref):
    out_ref[...] = jnp.where(lax.axis_index("ka") < 4, own_ref[...], in1_ref[...] + in2_ref[...] + in3_ref[...])


def fetch_kernel(*refs):
    count = len(refs) // 2
    copies = [pltpu.make_async_copy(refs[i], refs[count + i], refs[-1].at[i]) for i in range(count)]
    for copy in copies:
        copy.start()
    for copy in copies:
        copy.wait()


def density_kernel(home_ref, far_ref, fit_ref, out_ref, pair_ref):
    width = fit_ref.shape[1]
    for kind in range(2):
        for a in range(2):
            top = a * 16 + kind * 8
            home_r = home_ref[top : top + 8, :].astype(F32)[:, None, :]
            home_i = home_ref[32 + top : 40 + top, :].astype(F32)[:, None, :]
            for b in range(2):
                top = b * 16 + kind * 8
                far_r = far_ref[top : top + 8, :].astype(F32)[None]
                far_i = far_ref[32 + top : 40 + top, :].astype(F32)[None]
                real = (home_r * far_r + home_i * far_i).reshape(64, 256).astype(BF16)
                imag = (home_r * far_i - home_i * far_r).reshape(64, 256).astype(BF16)
                at = (a * 2 + b) * 64
                pair_ref[at : at + 64, 0:256] = real
                pair_ref[at : at + 64, 256:512] = -imag
                pair_ref[256 + at : 320 + at, 0:256] = imag
                pair_ref[256 + at : 320 + at, 256:512] = real
        for part in range(2):
            out_ref[kind, :, part * width : (part + 1) * width] = jnp.dot(
                pair_ref[part * 256 : (part + 1) * 256, :], fit_ref[...], preferred_element_type=F32
            ).astype(BF16)


def mixing_kernel(
    table_ref, row0_ref, row1_ref, row2_ref, row3_ref, density1_ref, density2_ref, density3_ref, out_ref, weight_ref
):
    width = weight_ref.shape[1] // 2
    place = lax.rem(lax.axis_index("ka"), 4)
    sent = [ref[...] for ref in (row0_ref, row1_ref, row2_ref, row3_ref)]
    for step, density_ref in enumerate((density1_ref, density2_ref, density3_ref)):
        away = place ^ (step + 1)
        rows = jnp.where(away == 0, sent[0], jnp.where(away == 1, sent[1], jnp.where(away == 2, sent[2], sent[3])))
        stored = [rows[q : q + 1] for q in range(2)]
        for a in range(2):
            blocks = []
            for b in range(2):
                screen = jnp.where(table_ref[a, b] == 0, stored[0], stored[1])
                at = (a * 2 + b) * 64
                val_r = density_ref[0, at : at + 64, 0:width].astype(F32)
                val_i = density_ref[0, at : at + 64, width:].astype(F32)
                weight_r = (val_r * screen).astype(BF16)
                weight_i = (val_i * screen).astype(BF16)
                weight_ref[0:64, 0:width] = weight_r
                weight_ref[0:64, width:] = weight_i
                weight_ref[64:128, 0:width] = weight_i
                weight_ref[64:128, width:] = -weight_r
                block = lax.dot_general(
                    density_ref[1, at : at + 64, :], weight_ref[...], (((1,), (1,)), ((), ())),
                    preferred_element_type=F32,
                )
                blocks.append(block.reshape(8, 8, 128))
            both = jnp.concatenate(blocks, axis=1).astype(BF16)
            for c in range(8):
                out_ref[a * 8 + c, step * 16 : (step + 1) * 16, :] = both[c]


def final_kernel(in_ref, out_ref):
    sublane = lax.broadcasted_iota(jnp.int32, (8, 128), 0)
    lane = lax.broadcasted_iota(jnp.int32, (8, 128), 1) // 8
    for step in range(STEPS):
        total = in_ref[0, step * 16 : (step + 1) * 16, :].astype(F32)
        for source in range(1, 16):
            total = total + in_ref[source, step * 16 : (step + 1) * 16, :].astype(F32)
        sides = []
        for b in range(2):
            x = total[b * 8 : (b + 1) * 8]
            for k in range(3):
                bit = 1 << k
                low = (sublane & bit) == 0
                low_lane = (lane & bit) == 0
                from_below = pltpu.roll(pltpu.roll(x, 8 - bit, 0), 8 * bit, 1)
                from_above = pltpu.roll(pltpu.roll(x, bit, 0), 128 - 8 * bit, 1)
                x = jnp.where(low == low_lane, x, jnp.where(low, from_below, from_above))
            sides.append(x)
        first_half = lane < 8
        out_ref[0, step] = jnp.where(first_half, sides[0], pltpu.roll(sides[1], 64, 1))
        out_ref[1, step] = jnp.where(first_half, pltpu.roll(sides[0], 64, 1), sides[1])


def body(orbitals, fit_vectors, screening, qpoint_table):
    vmem, smem = pltpu.VMEM, pltpu.SMEM
    width = fit_vectors.shape[2]

    def shifted(x, by, sources=range(16)):
        return lax.ppermute(x, "ka", [(i, (i + by) % 16) for i in sources])

    screen = screening[0]
    orbitals = orbitals.reshape(64, 256)
    far = [shifted(orbitals, by) for by in range(1, STEPS + 1)]
    screens = [shifted(screen, by, range(1, STEPS + 1)) for by in (4, 8, 12)]
    given = (fit_vectors.reshape(512, width), orbitals, screen)
    fit, home, screen = call(
        fetch_kernel, [(x.shape, x.dtype) for x in given],
        [pltpu.with_memory_space_constraint(x, pltpu.HBM) for x in given],
        (pltpu.HBM,) * 3, [pltpu.SemaphoreType.DMA((3,))], moved=1_700_000,
    )
    (row,) = call(row_kernel, [((2, width), F32)], (screen, *screens), (vmem,) * 4)
    rows = [row] + [lax.ppermute(row, "ka", [(i, i ^ mask) for i in range(16)]) for mask in (1, 2, 3)]
    densities = [
        call(
            density_kernel, [((2, 256, 2 * width), BF16)], (home, x, fit), (vmem,) * 3,
            [pltpu.VMEM((512, 512), BF16)], flops=2 * 8 * 256 * 256 * width, moved=2_000_000,
        )[0]
        for x in far
    ]
    (parts,) = call(
        mixing_kernel,
        [((16, 48, 128), BF16)],
        (qpoint_table, *rows, *densities),
        (smem,) + (vmem,) * 7,
        [pltpu.VMEM((128, 2 * width), BF16)],
        flops=2 * STEPS * 4 * 4 * 64 * 64 * width,
        moved=6_000_000,
    )
    parts = lax.all_to_all(parts, "ga", 0, 0)
    (out,) = call(final_kernel, [((2, STEPS, 8, 128), F32)], (parts,), (vmem,))
    return out[:, :, None]


def solution(mesh):
    in_specs = (P(None, "ka", None, None, None), P(None, None, "ga"), P("ka", None, "ga"), P())
    out_specs = P(None, None, "ka", "ga", None)
    return jax.shard_map(body, mesh=mesh, in_specs=in_specs, out_specs=out_specs, check_vma=False)
```

```python
import functools

import jax
import jax.numpy as jnp
from jax import lax
from jax.experimental import pallas as pl
from jax.experimental.pallas import tpu as pltpu
from jax.sharding import PartitionSpec as P

NV = 8
STEPS = 3
BF16 = jnp.bfloat16
F32 = jnp.float32
VMEM_LIMIT = 10 * 1024 * 1024


def call(kernel, out_shapes, operands, spaces, scratch=(), flops=0, moved=0):
    specs = [pl.BlockSpec(memory_space=space) for space in spaces]
    out_specs = [pl.BlockSpec(memory_space=pltpu.VMEM) for _ in out_shapes]
    return pl.pallas_call(
        kernel,
        out_shape=[jax.ShapeDtypeStruct(shape, kind) for shape, kind in out_shapes],
        in_specs=specs,
        out_specs=out_specs,
        scratch_shapes=list(scratch),
        compiler_params=pltpu.CompilerParams(vmem_limit_bytes=VMEM_LIMIT),
        cost_estimate=pl.CostEstimate(flops=flops, bytes_accessed=moved, transcendentals=0),
    )(*operands)


def row_kernel(span, held_ref, come_ref, out_ref):
    held = lax.rem(lax.axis_index("ka"), 2 * span) < span
    out_ref[...] = jnp.where(held, held_ref[...], come_ref[...])


def fetch_kernel(*refs):
    count = len(refs) // 2
    copies = [pltpu.make_async_copy(refs[i], refs[count + i], refs[-1].at[i]) for i in range(count)]
    for copy in copies:
        copy.start()
    for copy in copies:
        copy.wait()


def density_kernel(home_ref, far_ref, fit_ref, out_ref, pair_ref):
    width = fit_ref.shape[1]
    for kind in range(2):
        for a in range(2):
            top = a * 16 + kind * 8
            home_r = home_ref[top : top + 8, :].astype(F32)[:, None, :]
            home_i = home_ref[32 + top : 40 + top, :].astype(F32)[:, None, :]
            for b in range(2):
                top = b * 16 + kind * 8
                far_r = far_ref[top : top + 8, :].astype(F32)[None]
                far_i = far_ref[32 + top : 40 + top, :].astype(F32)[None]
                real = (home_r * far_r + home_i * far_i).reshape(64, 256).astype(BF16)
                imag = (home_r * far_i - home_i * far_r).reshape(64, 256).astype(BF16)
                at = (a * 2 + b) * 64
                pair_ref[at : at + 64, 0:256] = real
                pair_ref[at : at + 64, 256:512] = -imag
                pair_ref[256 + at : 320 + at, 0:256] = imag
                pair_ref[256 + at : 320 + at, 256:512] = real
        for part in range(2):
            out_ref[kind, :, part * width : (part + 1) * width] = jnp.dot(
                pair_ref[part * 256 : (part + 1) * 256, :], fit_ref[...], preferred_element_type=F32
            ).astype(BF16)


def mixing_kernel(
    table_ref, row0_ref, row1_ref, row2_ref, row3_ref, density1_ref, density2_ref, density3_ref, out_ref, weight_ref
):
    width = weight_ref.shape[1] // 2
    place = lax.rem(lax.axis_index("ka"), 4)
    sent = [ref[...] for ref in (row0_ref, row1_ref, row2_ref, row3_ref)]
    for step, density_ref in enumerate((density1_ref, density2_ref, density3_ref)):
        away = place ^ (step + 1)
        rows = jnp.where(away == 0, sent[0], jnp.where(away == 1, sent[1], jnp.where(away == 2, sent[2], sent[3])))
        stored = [rows[q : q + 1] for q in range(2)]
        for a in range(2):
            blocks = []
            for b in range(2):
                screen = jnp.where(table_ref[a, b] == 0, stored[0], stored[1])
                at = (a * 2 + b) * 64
                val_r = density_ref[0, at : at + 64, 0:width].astype(F32)
                val_i = density_ref[0, at : at + 64, width:].astype(F32)
                weight_r = (val_r * screen).astype(BF16)
                weight_i = (val_i * screen).astype(BF16)
                weight_ref[0:64, 0:width] = weight_r
                weight_ref[0:64, width:] = weight_i
                weight_ref[64:128, 0:width] = weight_i
                weight_ref[64:128, width:] = -weight_r
                block = lax.dot_general(
                    density_ref[1, at : at + 64, :], weight_ref[...], (((1,), (1,)), ((), ())),
                    preferred_element_type=F32,
                )
                blocks.append(block.reshape(8, 8, 128))
            both = jnp.concatenate(blocks, axis=1).astype(BF16)
            for c in range(8):
                out_ref[a * 8 + c, step * 16 : (step + 1) * 16, :] = both[c]


def final_kernel(in_ref, out_ref):
    sublane = lax.broadcasted_iota(jnp.int32, (8, 128), 0)
    lane = lax.broadcasted_iota(jnp.int32, (8, 128), 1) // 8
    for step in range(STEPS):
        total = in_ref[0, step * 16 : (step + 1) * 16, :].astype(F32)
        for source in range(1, 16):
            total = total + in_ref[source, step * 16 : (step + 1) * 16, :].astype(F32)
        sides = []
        for b in range(2):
            x = total[b * 8 : (b + 1) * 8]
            for k in range(3):
                bit = 1 << k
                low = (sublane & bit) == 0
                low_lane = (lane & bit) == 0
                from_below = pltpu.roll(pltpu.roll(x, 8 - bit, 0), 8 * bit, 1)
                from_above = pltpu.roll(pltpu.roll(x, bit, 0), 128 - 8 * bit, 1)
                x = jnp.where(low == low_lane, x, jnp.where(low, from_below, from_above))
            sides.append(x)
        first_half = lane < 8
        out_ref[0, step] = jnp.where(first_half, sides[0], pltpu.roll(sides[1], 64, 1))
        out_ref[1, step] = jnp.where(first_half, pltpu.roll(sides[0], 64, 1), sides[1])


def body(orbitals, fit_vectors, screening, qpoint_table):
    vmem, smem = pltpu.VMEM, pltpu.SMEM
    width = fit_vectors.shape[2]

    def shifted(x, by, sources=range(16)):
        return lax.ppermute(x, "ka", [(i, (i + by) % 16) for i in sources])

    screen = screening[0]
    orbitals = orbitals.reshape(64, 256)
    far = [shifted(orbitals, by) for by in range(1, STEPS + 1)]
    given = (fit_vectors.reshape(512, width), orbitals, screen)
    fit, home, screen = call(
        fetch_kernel, [(x.shape, x.dtype) for x in given],
        [pltpu.with_memory_space_constraint(x, pltpu.HBM) for x in given],
        (pltpu.HBM,) * 3, [pltpu.SemaphoreType.DMA((3,))], moved=1_700_000,
    )
    come = shifted(screening[0], 8, (1, 2, 3))
    (row,) = call(functools.partial(row_kernel, 8), [((2, width), F32)], (screen, come), (vmem,) * 2)
    come = shifted(row, 4, (1, 2, 3, 9, 10, 11))
    (row,) = call(functools.partial(row_kernel, 4), [((2, width), F32)], (row, come), (vmem,) * 2)
    rows = [row] + [lax.ppermute(row, "ka", [(i, i ^ mask) for i in range(16)]) for mask in (1, 2, 3)]
    densities = [
        call(
            density_kernel, [((2, 256, 2 * width), BF16)], (home, x, fit), (vmem,) * 3,
            [pltpu.VMEM((512, 512), BF16)], flops=2 * 8 * 256 * 256 * width, moved=2_000_000,
        )[0]
        for x in far
    ]
    (parts,) = call(
        mixing_kernel,
        [((16, 48, 128), BF16)],
        (qpoint_table, *rows, *densities),
        (smem,) + (vmem,) * 7,
        [pltpu.VMEM((128, 2 * width), BF16)],
        flops=2 * STEPS * 4 * 4 * 64 * 64 * width,
        moved=6_000_000,
    )
    parts = lax.all_to_all(parts, "ga", 0, 0)
    (out,) = call(final_kernel, [((2, STEPS, 8, 128), F32)], (parts,), (vmem,))
    return out[:, :, None]


def solution(mesh):
    in_specs = (P(None, "ka", None, None, None), P(None, None, "ga"), P("ka", None, "ga"), P())
    out_specs = P(None, None, "ka", "ga", None)
    return jax.shard_map(body, mesh=mesh, in_specs=in_specs, out_specs=out_specs, check_vma=False)
```

```python
import jax
import jax.numpy as jnp
from jax import lax
from jax.experimental import pallas as pl
from jax.experimental.pallas import tpu as pltpu
from jax.sharding import PartitionSpec as P

NV = 8
STEPS = 3
BF16 = jnp.bfloat16
F32 = jnp.float32
VMEM_LIMIT = 10 * 1024 * 1024


def call(kernel, out_shapes, operands, spaces, scratch=(), flops=0, moved=0):
    specs = [pl.BlockSpec(memory_space=space) for space in spaces]
    out_specs = [pl.BlockSpec(memory_space=pltpu.VMEM) for _ in out_shapes]
    return pl.pallas_call(
        kernel,
        out_shape=[jax.ShapeDtypeStruct(shape, kind) for shape, kind in out_shapes],
        in_specs=specs,
        out_specs=out_specs,
        scratch_shapes=list(scratch),
        compiler_params=pltpu.CompilerParams(vmem_limit_bytes=VMEM_LIMIT),
        cost_estimate=pl.CostEstimate(flops=flops, bytes_accessed=moved, transcendentals=0),
    )(*operands)


def payload_kernel(screen_ref, orbital_ref, out_ref, home_ref, screen_scr, sems):
    first = pltpu.make_async_copy(screen_ref, screen_scr, sems.at[0])
    second = pltpu.make_async_copy(orbital_ref, home_ref, sems.at[1])
    first.start()
    second.start()
    first.wait()
    pieces = []
    for q in range(2):
        for j in range(3):
            pieces.append(screen_scr[q : q + 1, 256 * j : 256 * (j + 1)])
    rows = jnp.concatenate(pieces + [jnp.zeros((2, 256), F32)], axis=0)
    high = rows.astype(BF16)
    low = (rows - high.astype(F32)).astype(BF16)
    block = jnp.concatenate([high.astype(F32), low.astype(F32)], axis=0).astype(BF16)
    for target in range(16):
        out_ref[target] = block
    second.wait()


def fetch_kernel(fit_ref, home_ref, ready_ref, fit_out_ref, home_out_ref, sems):
    first = pltpu.make_async_copy(fit_ref, fit_out_ref, sems.at[0])
    second = pltpu.make_async_copy(home_ref, home_out_ref, sems.at[1])
    first.start()
    second.start()
    first.wait()
    second.wait()


def density_kernel(home_ref, far_ref, fit_ref, ready_ref, out_ref, pair_ref):
    width = fit_ref.shape[1]
    for kind in range(2):
        for a in range(2):
            top = a * 16 + kind * 8
            home_r = home_ref[top : top + 8, :].astype(F32)[:, None, :]
            home_i = home_ref[32 + top : 40 + top, :].astype(F32)[:, None, :]
            for b in range(2):
                top = b * 16 + kind * 8
                far_r = far_ref[top : top + 8, :].astype(F32)[None]
                far_i = far_ref[32 + top : 40 + top, :].astype(F32)[None]
                real = (home_r * far_r + home_i * far_i).reshape(64, 256).astype(BF16)
                imag = (home_r * far_i - home_i * far_r).reshape(64, 256).astype(BF16)
                at = (a * 2 + b) * 64
                pair_ref[at : at + 64, 0:256] = real
                pair_ref[at : at + 64, 256:512] = -imag
                pair_ref[256 + at : 320 + at, 0:256] = imag
                pair_ref[256 + at : 320 + at, 256:512] = real
        for part in range(2):
            out_ref[kind, :, part * width : (part + 1) * width] = jnp.dot(
                pair_ref[part * 256 : (part + 1) * 256, :], fit_ref[...], preferred_element_type=F32
            ).astype(BF16)


def mixing_kernel(
    table_ref, screen_ref, density1_ref, density2_ref, density3_ref, out_ref, weight_ref
):
    width = weight_ref.shape[1] // 2
    for step, density_ref in enumerate((density1_ref, density2_ref, density3_ref)):
        rows = screen_ref[step + 1].astype(F32)
        rows = rows[0:8] + rows[8:16]
        stored = [
            jnp.concatenate([rows[3 * q + j : 3 * q + j + 1] for j in range(3)], axis=1) for q in range(2)
        ]
        for a in range(2):
            blocks = []
            for b in range(2):
                screen = jnp.where(table_ref[a, b] == 0, stored[0], stored[1])
                at = (a * 2 + b) * 64
                val_r = density_ref[0, at : at + 64, 0:width].astype(F32)
                val_i = density_ref[0, at : at + 64, width:].astype(F32)
                weight_r = (val_r * screen).astype(BF16)
                weight_i = (val_i * screen).astype(BF16)
                weight_ref[0:64, 0:width] = weight_r
                weight_ref[0:64, width:] = weight_i
                weight_ref[64:128, 0:width] = weight_i
                weight_ref[64:128, width:] = -weight_r
                block = lax.dot_general(
                    density_ref[1, at : at + 64, :], weight_ref[...], (((1,), (1,)), ((), ())),
                    preferred_element_type=F32,
                )
                blocks.append(block.reshape(8, 8, 128))
            both = jnp.concatenate(blocks, axis=1).astype(BF16)
            for c in range(8):
                out_ref[a * 8 + c, step * 16 : (step + 1) * 16, :] = both[c]


def final_kernel(in_ref, out_ref):
    sublane = lax.broadcasted_iota(jnp.int32, (8, 128), 0)
    lane = lax.broadcasted_iota(jnp.int32, (8, 128), 1) // 8
    for step in range(STEPS):
        total = in_ref[0, step * 16 : (step + 1) * 16, :].astype(F32)
        for source in range(1, 16):
            total = total + in_ref[source, step * 16 : (step + 1) * 16, :].astype(F32)
        sides = []
        for b in range(2):
            x = total[b * 8 : (b + 1) * 8]
            for k in range(3):
                bit = 1 << k
                low = (sublane & bit) == 0
                low_lane = (lane & bit) == 0
                from_below = pltpu.roll(pltpu.roll(x, 8 - bit, 0), 8 * bit, 1)
                from_above = pltpu.roll(pltpu.roll(x, bit, 0), 128 - 8 * bit, 1)
                x = jnp.where(low == low_lane, x, jnp.where(low, from_below, from_above))
            sides.append(x)
        first_half = lane < 8
        out_ref[0, step] = jnp.where(first_half, sides[0], pltpu.roll(sides[1], 64, 1))
        out_ref[1, step] = jnp.where(first_half, pltpu.roll(sides[0], 64, 1), sides[1])


def body(orbitals, fit_vectors, screening, qpoint_table):
    vmem, smem = pltpu.VMEM, pltpu.SMEM
    width = fit_vectors.shape[2]

    def shifted(x, by, sources=range(16)):
        return lax.ppermute(x, "ka", [(i, (i + by) % 16) for i in sources])

    hbm = pltpu.HBM
    given = [pltpu.with_memory_space_constraint(x, hbm) for x in (screening[0], orbitals.reshape(64, 256))]
    payload, home = call(
        payload_kernel, [((16, 16, 256), BF16), ((64, 256), BF16)], given, (hbm, hbm),
        [pltpu.VMEM((2, width), F32), pltpu.SemaphoreType.DMA((2,))], moved=200_000,
    )
    screens = lax.all_to_all(payload, "ka", 0, 0)
    far = [shifted(home, by) for by in range(1, STEPS + 1)]
    fit, home = call(
        fetch_kernel, [((512, width), BF16), ((64, 256), BF16)],
        [
            pltpu.with_memory_space_constraint(x, hbm)
            for x in (fit_vectors.reshape(512, width), orbitals.reshape(64, 256))
        ] + [screens],
        (hbm, hbm, pl.ANY), [pltpu.SemaphoreType.DMA((2,))], moved=1_700_000,
    )
    densities = [
        call(
            density_kernel, [((2, 256, 2 * width), BF16)], (home, x, fit, screens), (vmem,) * 3 + (pl.ANY,),
            [pltpu.VMEM((512, 512), BF16)], flops=2 * 8 * 256 * 256 * width, moved=2_000_000,
        )[0]
        for x in far
    ]
    (parts,) = call(
        mixing_kernel,
        [((16, 48, 128), BF16)],
        (qpoint_table, screens, *densities),
        (smem,) + (vmem,) * 4,
        [pltpu.VMEM((128, 2 * width), BF16)],
        flops=2 * STEPS * 4 * 4 * 64 * 64 * width,
        moved=6_000_000,
    )
    parts = lax.all_to_all(parts, "ga", 0, 0)
    (out,) = call(final_kernel, [((2, STEPS, 8, 128), F32)], (parts,), (vmem,))
    return out[:, :, None]


def solution(mesh):
    in_specs = (P(None, "ka", None, None, None), P(None, None, "ga"), P("ka", None, "ga"), P())
    out_specs = P(None, None, "ka", "ga", None)
    return jax.shard_map(body, mesh=mesh, in_specs=in_specs, out_specs=out_specs, check_vma=False)
```

```python
import jax
import jax.numpy as jnp
from jax import lax
from jax.experimental import pallas as pl
from jax.experimental.pallas import tpu as pltpu
from jax.sharding import PartitionSpec as P

NV = 8
STEPS = 3
BF16 = jnp.bfloat16
F32 = jnp.float32
VMEM_LIMIT = 24 * 1024 * 1024


def call(kernel, out_shapes, operands, spaces, scratch=(), flops=0, moved=0):
    specs = [pl.BlockSpec(memory_space=space) for space in spaces]
    out_specs = [pl.BlockSpec(memory_space=pltpu.VMEM) for _ in out_shapes]
    return pl.pallas_call(
        kernel,
        out_shape=[jax.ShapeDtypeStruct(shape, kind) for shape, kind in out_shapes],
        in_specs=specs,
        out_specs=out_specs,
        scratch_shapes=list(scratch),
        compiler_params=pltpu.CompilerParams(vmem_limit_bytes=VMEM_LIMIT),
        cost_estimate=pl.CostEstimate(flops=flops, bytes_accessed=moved, transcendentals=0),
    )(*operands)


def payload_kernel(screen_ref, orbital_ref, out_ref, home_ref, screen_scr, sems):
    first = pltpu.make_async_copy(screen_ref, screen_scr, sems.at[0])
    second = pltpu.make_async_copy(orbital_ref, home_ref, sems.at[1])
    first.start()
    second.start()
    first.wait()
    pieces = []
    for q in range(2):
        for j in range(3):
            pieces.append(screen_scr[q : q + 1, 256 * j : 256 * (j + 1)])
    rows = jnp.concatenate(pieces + [jnp.zeros((2, 256), F32)], axis=0)
    high = rows.astype(BF16)
    low = (rows - high.astype(F32)).astype(BF16)
    block = jnp.concatenate([high.astype(F32), low.astype(F32)], axis=0).astype(BF16)
    for target in range(16):
        out_ref[target] = block
    second.wait()


def pair_products(home_ref, far_ref, kind, out_ref):
    for a in range(2):
        top = a * 16 + kind * 8
        home_r = home_ref[top : top + 8, :].astype(F32)[:, None, :]
        home_i = home_ref[32 + top : 40 + top, :].astype(F32)[:, None, :]
        for b in range(2):
            top = b * 16 + kind * 8
            far_r = far_ref[top : top + 8, :].astype(F32)[None]
            far_i = far_ref[32 + top : 40 + top, :].astype(F32)[None]
            real = (home_r * far_r + home_i * far_i).reshape(64, 256).astype(BF16)
            imag = (home_r * far_i - home_i * far_r).reshape(64, 256).astype(BF16)
            at = (a * 2 + b) * 64
            out_ref[at : at + 64, 0:256] = real
            out_ref[at : at + 64, 256:512] = -imag
            out_ref[256 + at : 320 + at, 0:256] = imag
            out_ref[256 + at : 320 + at, 256:512] = real


def block_kernel(
    table_ref, orbital_ref, far1_ref, far2_ref, far3_ref, fit_hbm_ref, screen_ref, out_ref,
    home_ref, fit_ref, pair_ref, density_ref, weight_ref, sems,
):
    width = fit_ref.shape[1]
    home_copy = pltpu.make_async_copy(orbital_ref, home_ref, sems.at[0])
    fit_copy = pltpu.make_async_copy(fit_hbm_ref, fit_ref, sems.at[1])
    home_copy.start()
    fit_copy.start()
    home_copy.wait()
    fars = (far1_ref, far2_ref, far3_ref)
    for step in range(STEPS):
        for kind in range(2):
            pair_products(home_ref, fars[step], kind, pair_ref.at[step, kind])
    fit_copy.wait()
    for step in range(STEPS):
        for kind in range(2):
            for part in range(2):
                density_ref[step, kind, :, part * width : (part + 1) * width] = jnp.dot(
                    pair_ref[step, kind, part * 256 : (part + 1) * 256, :], fit_ref[...], preferred_element_type=F32
                ).astype(BF16)
        rows = screen_ref[step + 1].astype(F32)
        rows = rows[0:8] + rows[8:16]
        stored = [
            jnp.concatenate([rows[3 * q + j : 3 * q + j + 1] for j in range(3)], axis=1) for q in range(2)
        ]
        for a in range(2):
            blocks = []
            for b in range(2):
                screen = jnp.where(table_ref[a, b] == 0, stored[0], stored[1])
                at = (a * 2 + b) * 64
                val_r = density_ref[step, 0, at : at + 64, 0:width].astype(F32)
                val_i = density_ref[step, 0, at : at + 64, width:].astype(F32)
                weight_r = (val_r * screen).astype(BF16)
                weight_i = (val_i * screen).astype(BF16)
                slot = (step * 2 + a) * 2 + b
                weight_ref[slot, 0:64, 0:width] = weight_r
                weight_ref[slot, 0:64, width:] = weight_i
                weight_ref[slot, 64:128, 0:width] = weight_i
                weight_ref[slot, 64:128, width:] = -weight_r
                block = lax.dot_general(
                    density_ref[step, 1, at : at + 64, :], weight_ref[slot], (((1,), (1,)), ((), ())),
                    preferred_element_type=F32,
                )
                blocks.append(block.reshape(8, 8, 128))
            both = jnp.concatenate(blocks, axis=1).astype(BF16)
            for c in range(8):
                out_ref[a * 8 + c, step * 16 : (step + 1) * 16, :] = both[c]


def final_kernel(in_ref, out_ref):
    sublane = lax.broadcasted_iota(jnp.int32, (8, 128), 0)
    lane = lax.broadcasted_iota(jnp.int32, (8, 128), 1) // 8
    for step in range(STEPS):
        total = in_ref[0, step * 16 : (step + 1) * 16, :].astype(F32)
        for source in range(1, 16):
            total = total + in_ref[source, step * 16 : (step + 1) * 16, :].astype(F32)
        sides = []
        for b in range(2):
            x = total[b * 8 : (b + 1) * 8]
            for k in range(3):
                bit = 1 << k
                low = (sublane & bit) == 0
                low_lane = (lane & bit) == 0
                from_below = pltpu.roll(pltpu.roll(x, 8 - bit, 0), 8 * bit, 1)
                from_above = pltpu.roll(pltpu.roll(x, bit, 0), 128 - 8 * bit, 1)
                x = jnp.where(low == low_lane, x, jnp.where(low, from_below, from_above))
            sides.append(x)
        first_half = lane < 8
        out_ref[0, step] = jnp.where(first_half, sides[0], pltpu.roll(sides[1], 64, 1))
        out_ref[1, step] = jnp.where(first_half, pltpu.roll(sides[0], 64, 1), sides[1])


def body(orbitals, fit_vectors, screening, qpoint_table):
    vmem, smem = pltpu.VMEM, pltpu.SMEM
    width = fit_vectors.shape[2]

    def shifted(x, by, sources=range(16)):
        return lax.ppermute(x, "ka", [(i, (i + by) % 16) for i in sources])

    hbm = pltpu.HBM
    given = [pltpu.with_memory_space_constraint(x, hbm) for x in (screening[0], orbitals.reshape(64, 256))]
    payload, home = call(
        payload_kernel, [((16, 16, 256), BF16), ((64, 256), BF16)], given, (hbm, hbm),
        [pltpu.VMEM((2, width), F32), pltpu.SemaphoreType.DMA((2,))], moved=200_000,
    )
    screens = lax.all_to_all(payload, "ka", 0, 0)
    far = [shifted(home, by) for by in range(1, STEPS + 1)]
    (parts,) = call(
        block_kernel,
        [((16, 48, 128), BF16)],
        (
            qpoint_table, given[1], *far,
            pltpu.with_memory_space_constraint(fit_vectors.reshape(512, width), hbm), screens,
        ),
        (smem, hbm, vmem, vmem, vmem, hbm, vmem),
        [
            pltpu.VMEM((64, 256), BF16), pltpu.VMEM((512, width), BF16), pltpu.VMEM((STEPS, 2, 512, 512), BF16),
            pltpu.VMEM((STEPS, 2, 256, 2 * width), BF16), pltpu.VMEM((4 * STEPS, 128, 2 * width), BF16),
            pltpu.SemaphoreType.DMA((2,)),
        ],
        flops=2 * STEPS * (8 * 256 * 256 + 4 * 4 * 64 * 64) * width,
        moved=3_000_000,
    )
    parts = lax.all_to_all(parts, "ga", 0, 0)
    (out,) = call(final_kernel, [((2, STEPS, 8, 128), F32)], (parts,), (vmem,))
    return out[:, :, None]


def solution(mesh):
    in_specs = (P(None, "ka", None, None, None), P(None, None, "ga"), P("ka", None, "ga"), P())
    out_specs = P(None, None, "ka", "ga", None)
    return jax.shard_map(body, mesh=mesh, in_specs=in_specs, out_specs=out_specs, check_vma=False)
```

```python
import jax
import jax.numpy as jnp
from jax import lax
from jax.experimental import pallas as pl
from jax.experimental.pallas import tpu as pltpu
from jax.sharding import PartitionSpec as P

NV = 8
STEPS = 3
BF16 = jnp.bfloat16
F32 = jnp.float32
VMEM_LIMIT = 24 * 1024 * 1024


def call(kernel, out_shapes, operands, spaces, scratch=(), flops=0, moved=0):
    specs = [pl.BlockSpec(memory_space=space) for space in spaces]
    out_specs = [pl.BlockSpec(memory_space=pltpu.VMEM) for _ in out_shapes]
    return pl.pallas_call(
        kernel,
        out_shape=[jax.ShapeDtypeStruct(shape, kind) for shape, kind in out_shapes],
        in_specs=specs,
        out_specs=out_specs,
        scratch_shapes=list(scratch),
        compiler_params=pltpu.CompilerParams(vmem_limit_bytes=VMEM_LIMIT),
        cost_estimate=pl.CostEstimate(flops=flops, bytes_accessed=moved, transcendentals=0),
    )(*operands)


def payload_kernel(screen_ref, out_ref, held_ref, sem):
    copy = pltpu.make_async_copy(screen_ref, held_ref, sem)
    copy.start()
    copy.wait()
    pieces = []
    for q in range(2):
        for j in range(3):
            pieces.append(held_ref[q : q + 1, 256 * j : 256 * (j + 1)])
    rows = jnp.concatenate(pieces + [jnp.zeros((2, 256), F32)], axis=0)
    high = rows.astype(BF16)
    low = (rows - high.astype(F32)).astype(BF16)
    block = jnp.concatenate([high.astype(F32), low.astype(F32)], axis=0).astype(BF16)
    for target in range(16):
        out_ref[target] = block


def pair_products(home_ref, far_ref, kind, out_ref):
    for a in range(2):
        top = a * 16 + kind * 8
        home_r = home_ref[top : top + 8, :].astype(F32)[:, None, :]
        home_i = home_ref[32 + top : 40 + top, :].astype(F32)[:, None, :]
        for b in range(2):
            top = b * 16 + kind * 8
            far_r = far_ref[top : top + 8, :].astype(F32)[None]
            far_i = far_ref[32 + top : 40 + top, :].astype(F32)[None]
            real = (home_r * far_r + home_i * far_i).reshape(64, 256).astype(BF16)
            imag = (home_r * far_i - home_i * far_r).reshape(64, 256).astype(BF16)
            at = (a * 2 + b) * 64
            out_ref[at : at + 64, 0:256] = real
            out_ref[at : at + 64, 256:512] = -imag
            out_ref[256 + at : 320 + at, 0:256] = imag
            out_ref[256 + at : 320 + at, 256:512] = real


def density_rows(pair_ref, fit_ref, out_ref):
    width = fit_ref.shape[1]
    for part in range(2):
        out_ref[:, part * width : (part + 1) * width] = jnp.dot(
            pair_ref[part * 256 : (part + 1) * 256, :], fit_ref[...], preferred_element_type=F32
        ).astype(BF16)


def valence_kernel(
    orbital_ref, far1_ref, far2_ref, far3_ref, fit_hbm_ref, home_ref, fit_ref, val_ref, pair_ref, sems
):
    home_copy = pltpu.make_async_copy(orbital_ref, home_ref, sems.at[0])
    fit_copy = pltpu.make_async_copy(fit_hbm_ref, fit_ref, sems.at[1])
    home_copy.start()
    fit_copy.start()
    home_copy.wait()
    for step, far_ref in enumerate((far1_ref, far2_ref, far3_ref)):
        pair_products(home_ref, far_ref, 0, pair_ref.at[step])
    fit_copy.wait()
    for step in range(STEPS):
        density_rows(pair_ref.at[step], fit_ref, val_ref.at[step])


def block_kernel(
    table_ref, home_ref, far1_ref, far2_ref, far3_ref, fit_ref, val_ref, screen_ref, out_ref,
    pair_ref, cond_ref, weight_ref,
):
    width = fit_ref.shape[1]
    for step, far_ref in enumerate((far1_ref, far2_ref, far3_ref)):
        pair_products(home_ref, far_ref, 1, pair_ref.at[step])
        density_rows(pair_ref.at[step], fit_ref, cond_ref.at[step])
        rows = screen_ref[step + 1].astype(F32)
        rows = rows[0:8] + rows[8:16]
        stored = [
            jnp.concatenate([rows[3 * q + j : 3 * q + j + 1] for j in range(3)], axis=1) for q in range(2)
        ]
        for a in range(2):
            blocks = []
            for b in range(2):
                screen = jnp.where(table_ref[a, b] == 0, stored[0], stored[1])
                at = (a * 2 + b) * 64
                val_r = val_ref[step, at : at + 64, 0:width].astype(F32)
                val_i = val_ref[step, at : at + 64, width:].astype(F32)
                weight_r = (val_r * screen).astype(BF16)
                weight_i = (val_i * screen).astype(BF16)
                slot = (step * 2 + a) * 2 + b
                weight_ref[slot, 0:64, 0:width] = weight_r
                weight_ref[slot, 0:64, width:] = weight_i
                weight_ref[slot, 64:128, 0:width] = weight_i
                weight_ref[slot, 64:128, width:] = -weight_r
                block = lax.dot_general(
                    cond_ref[step, at : at + 64, :], weight_ref[slot], (((1,), (1,)), ((), ())),
                    preferred_element_type=F32,
                )
                blocks.append(block.reshape(8, 8, 128))
            both = jnp.concatenate(blocks, axis=1).astype(BF16)
            for c in range(8):
                out_ref[a * 8 + c, step * 16 : (step + 1) * 16, :] = both[c]


def final_kernel(in_ref, out_ref):
    sublane = lax.broadcasted_iota(jnp.int32, (8, 128), 0)
    lane = lax.broadcasted_iota(jnp.int32, (8, 128), 1) // 8
    for step in range(STEPS):
        total = in_ref[0, step * 16 : (step + 1) * 16, :].astype(F32)
        for source in range(1, 16):
            total = total + in_ref[source, step * 16 : (step + 1) * 16, :].astype(F32)
        sides = []
        for b in range(2):
            x = total[b * 8 : (b + 1) * 8]
            for k in range(3):
                bit = 1 << k
                low = (sublane & bit) == 0
                low_lane = (lane & bit) == 0
                from_below = pltpu.roll(pltpu.roll(x, 8 - bit, 0), 8 * bit, 1)
                from_above = pltpu.roll(pltpu.roll(x, bit, 0), 128 - 8 * bit, 1)
                x = jnp.where(low == low_lane, x, jnp.where(low, from_below, from_above))
            sides.append(x)
        first_half = lane < 8
        out_ref[0, step] = jnp.where(first_half, sides[0], pltpu.roll(sides[1], 64, 1))
        out_ref[1, step] = jnp.where(first_half, pltpu.roll(sides[0], 64, 1), sides[1])


def body(orbitals, fit_vectors, screening, qpoint_table):
    vmem, smem = pltpu.VMEM, pltpu.SMEM
    width = fit_vectors.shape[2]

    def shifted(x, by, sources=range(16)):
        return lax.ppermute(x, "ka", [(i, (i + by) % 16) for i in sources])

    hbm = pltpu.HBM
    orbitals = orbitals.reshape(64, 256)
    far = [shifted(orbitals, by) for by in range(1, STEPS + 1)]
    fit, home, screen = [
        pltpu.with_memory_space_constraint(x, hbm)
        for x in (fit_vectors.reshape(512, width), orbitals, screening[0])
    ]
    (payload,) = call(
        payload_kernel, [((16, 16, 256), BF16)], (screen,), (hbm,),
        [pltpu.VMEM((2, width), F32), pltpu.SemaphoreType.DMA], moved=200_000,
    )
    screens = lax.all_to_all(payload, "ka", 0, 0)
    home, fit, val = call(
        valence_kernel,
        [((64, 256), BF16), ((512, width), BF16), ((STEPS, 256, 2 * width), BF16)],
        (home, *far, fit), (hbm, vmem, vmem, vmem, hbm),
        [pltpu.VMEM((STEPS, 512, 512), BF16), pltpu.SemaphoreType.DMA((2,))],
        flops=2 * STEPS * 4 * 256 * 256 * width, moved=3_000_000,
    )
    (parts,) = call(
        block_kernel,
        [((16, 48, 128), BF16)],
        (qpoint_table, home, *far, fit, val, screens),
        (smem,) + (vmem,) * 7,
        [
            pltpu.VMEM((STEPS, 512, 512), BF16), pltpu.VMEM((STEPS, 256, 2 * width), BF16),
            pltpu.VMEM((4 * STEPS, 128, 2 * width), BF16),
        ],
        flops=2 * STEPS * (4 * 256 * 256 + 4 * 4 * 64 * 64) * width,
        moved=3_000_000,
    )
    parts = lax.all_to_all(parts, "ga", 0, 0)
    (out,) = call(final_kernel, [((2, STEPS, 8, 128), F32)], (parts,), (vmem,))
    return out[:, :, None]


def solution(mesh):
    in_specs = (P(None, "ka", None, None, None), P(None, None, "ga"), P("ka", None, "ga"), P())
    out_specs = P(None, None, "ka", "ga", None)
    return jax.shard_map(body, mesh=mesh, in_specs=in_specs, out_specs=out_specs, check_vma=False)
```

```python
import jax
import jax.numpy as jnp
from jax import lax
from jax.experimental import pallas as pl
from jax.experimental.pallas import tpu as pltpu
from jax.sharding import PartitionSpec as P

NV = 8
STEPS = 3
BF16 = jnp.bfloat16
F32 = jnp.float32
VMEM_LIMIT = 24 * 1024 * 1024


def call(kernel, out_shapes, operands, spaces, scratch=(), flops=0, moved=0):
    specs = [pl.BlockSpec(memory_space=space) for space in spaces]
    out_specs = [pl.BlockSpec(memory_space=pltpu.VMEM) for _ in out_shapes]
    return pl.pallas_call(
        kernel,
        out_shape=[jax.ShapeDtypeStruct(shape, kind) for shape, kind in out_shapes],
        in_specs=specs,
        out_specs=out_specs,
        scratch_shapes=list(scratch),
        compiler_params=pltpu.CompilerParams(vmem_limit_bytes=VMEM_LIMIT),
        cost_estimate=pl.CostEstimate(flops=flops, bytes_accessed=moved, transcendentals=0),
    )(*operands)


def payload_kernel(screen_ref, out_ref, held_ref, sem):
    copy = pltpu.make_async_copy(screen_ref, held_ref, sem)
    copy.start()
    copy.wait()
    pieces = []
    for q in range(2):
        for j in range(3):
            pieces.append(held_ref[q : q + 1, 256 * j : 256 * (j + 1)])
    rows = jnp.concatenate(pieces + [jnp.zeros((2, 256), F32)], axis=0)
    high = rows.astype(BF16)
    low = (rows - high.astype(F32)).astype(BF16)
    block = jnp.concatenate([high.astype(F32), low.astype(F32)], axis=0).astype(BF16)
    for target in range(16):
        out_ref[target] = block


def pair_products(home_ref, far_ref, kind, out_ref):
    for a in range(2):
        top = a * 16 + kind * 8
        home_r = home_ref[top : top + 8, :].astype(F32)[:, None, :]
        home_i = home_ref[32 + top : 40 + top, :].astype(F32)[:, None, :]
        for b in range(2):
            top = b * 16 + kind * 8
            far_r = far_ref[top : top + 8, :].astype(F32)[None]
            far_i = far_ref[32 + top : 40 + top, :].astype(F32)[None]
            real = (home_r * far_r + home_i * far_i).reshape(64, 256).astype(BF16)
            imag = (home_r * far_i - home_i * far_r).reshape(64, 256).astype(BF16)
            at = (a * 2 + b) * 128
            out_ref[at : at + 64, 0:256] = real
            out_ref[at : at + 64, 256:512] = -imag
            out_ref[at + 64 : at + 128, 0:256] = imag
            out_ref[at + 64 : at + 128, 256:512] = real


def density_rows(pair_ref, fit_ref, out_ref):
    for half in range(2):
        at = half * 256
        out_ref[at : at + 256, :] = jnp.dot(
            pair_ref[at : at + 256, :], fit_ref[...], preferred_element_type=F32
        ).astype(BF16)


def valence_kernel(
    orbital_ref, far1_ref, far2_ref, far3_ref, fit_hbm_ref, home_ref, fit_ref, val_ref, pair_ref, sems
):
    home_copy = pltpu.make_async_copy(orbital_ref, home_ref, sems.at[0])
    fit_copy = pltpu.make_async_copy(fit_hbm_ref, fit_ref, sems.at[1])
    home_copy.start()
    fit_copy.start()
    home_copy.wait()
    for step, far_ref in enumerate((far1_ref, far2_ref, far3_ref)):
        pair_products(home_ref, far_ref, 0, pair_ref.at[step])
    fit_copy.wait()
    for step in range(STEPS):
        density_rows(pair_ref.at[step], fit_ref, val_ref.at[step])


def block_kernel(
    table_ref, home_ref, far1_ref, far2_ref, far3_ref, fit_ref, val_ref, screen_ref, out_ref,
    pair_ref, cond_ref, weight_ref,
):
    first_half = lax.broadcasted_iota(jnp.int32, (64, 128), 1) < 64
    for step, far_ref in enumerate((far1_ref, far2_ref, far3_ref)):
        pair_products(home_ref, far_ref, 1, pair_ref.at[step])
        rows = screen_ref[step + 1].astype(F32)
        rows = rows[0:8] + rows[8:16]
        stored = [
            jnp.concatenate([rows[3 * q + j : 3 * q + j + 1] for j in range(3)], axis=1) for q in range(2)
        ]
        for a in range(2):
            for b in range(2):
                screen = jnp.where(table_ref[a, b] == 0, stored[0], stored[1])
                at = (a * 2 + b) * 128
                weight_ref[step, at : at + 128, :] = (val_ref[step, at : at + 128, :].astype(F32) * screen).astype(BF16)
        density_rows(pair_ref.at[step], fit_ref, cond_ref.at[step])
        for a in range(2):
            blocks = []
            for b in range(2):
                at = (a * 2 + b) * 128
                products = lax.dot_general(
                    cond_ref[step, at : at + 128, :], weight_ref[step, at : at + 128, :], (((1,), (1,)), ((), ())),
                    preferred_element_type=F32,
                )
                below = pltpu.roll(products[64:128], 64, 1)
                block = products[0:64] + jnp.where(first_half, below, -below)
                blocks.append(block.reshape(8, 8, 128))
            both = jnp.concatenate(blocks, axis=1).astype(BF16)
            for c in range(8):
                out_ref[a * 8 + c, step * 16 : (step + 1) * 16, :] = both[c]


def final_kernel(in_ref, out_ref):
    sublane = lax.broadcasted_iota(jnp.int32, (8, 128), 0)
    lane = lax.broadcasted_iota(jnp.int32, (8, 128), 1) // 8
    for step in range(STEPS):
        total = in_ref[0, step * 16 : (step + 1) * 16, :].astype(F32)
        for source in range(1, 16):
            total = total + in_ref[source, step * 16 : (step + 1) * 16, :].astype(F32)
        sides = []
        for b in range(2):
            x = total[b * 8 : (b + 1) * 8]
            for k in range(3):
                bit = 1 << k
                low = (sublane & bit) == 0
                low_lane = (lane & bit) == 0
                from_below = pltpu.roll(pltpu.roll(x, 8 - bit, 0), 8 * bit, 1)
                from_above = pltpu.roll(pltpu.roll(x, bit, 0), 128 - 8 * bit, 1)
                x = jnp.where(low == low_lane, x, jnp.where(low, from_below, from_above))
            sides.append(x)
        first_half = lane < 8
        out_ref[0, step] = jnp.where(first_half, sides[0], pltpu.roll(sides[1], 64, 1))
        out_ref[1, step] = jnp.where(first_half, pltpu.roll(sides[0], 64, 1), sides[1])


def body(orbitals, fit_vectors, screening, qpoint_table):
    vmem, smem = pltpu.VMEM, pltpu.SMEM
    width = fit_vectors.shape[2]

    def shifted(x, by, sources=range(16)):
        return lax.ppermute(x, "ka", [(i, (i + by) % 16) for i in sources])

    hbm = pltpu.HBM
    orbitals = orbitals.reshape(64, 256)
    far = [shifted(orbitals, by) for by in range(1, STEPS + 1)]
    fit, home, screen = [
        pltpu.with_memory_space_constraint(x, hbm)
        for x in (fit_vectors.reshape(512, width), orbitals, screening[0])
    ]
    (payload,) = call(
        payload_kernel, [((16, 16, 256), BF16)], (screen,), (hbm,),
        [pltpu.VMEM((2, width), F32), pltpu.SemaphoreType.DMA], moved=200_000,
    )
    screens = lax.all_to_all(payload, "ka", 0, 0)
    home, fit, val = call(
        valence_kernel,
        [((64, 256), BF16), ((512, width), BF16), ((STEPS, 512, width), BF16)],
        (home, *far, fit), (hbm, vmem, vmem, vmem, hbm),
        [pltpu.VMEM((STEPS, 512, 512), BF16), pltpu.SemaphoreType.DMA((2,))],
        flops=2 * STEPS * 4 * 256 * 256 * width, moved=3_000_000,
    )
    (parts,) = call(
        block_kernel,
        [((16, 48, 128), BF16)],
        (qpoint_table, home, *far, fit, val, screens),
        (smem,) + (vmem,) * 7,
        [
            pltpu.VMEM((STEPS, 512, 512), BF16), pltpu.VMEM((STEPS, 512, width), BF16),
            pltpu.VMEM((STEPS, 512, width), BF16),
        ],
        flops=2 * STEPS * (4 * 256 * 256 + 4 * 4 * 64 * 64) * width,
        moved=3_000_000,
    )
    parts = lax.all_to_all(parts, "ga", 0, 0)
    (out,) = call(final_kernel, [((2, STEPS, 8, 128), F32)], (parts,), (vmem,))
    return out[:, :, None]


def solution(mesh):
    in_specs = (P(None, "ka", None, None, None), P(None, None, "ga"), P("ka", None, "ga"), P())
    out_specs = P(None, None, "ka", "ga", None)
    return jax.shard_map(body, mesh=mesh, in_specs=in_specs, out_specs=out_specs, check_vma=False)
```

```python
import jax
import jax.numpy as jnp
from jax import lax
from jax.experimental import pallas as pl
from jax.experimental.pallas import tpu as pltpu
from jax.sharding import PartitionSpec as P

NV = 8
STEPS = 3
BF16 = jnp.bfloat16
F32 = jnp.float32
VMEM_LIMIT = 24 * 1024 * 1024


def call(kernel, out_shapes, operands, spaces, scratch=(), flops=0, moved=0):
    specs = [pl.BlockSpec(memory_space=space) for space in spaces]
    out_specs = [pl.BlockSpec(memory_space=pltpu.VMEM) for _ in out_shapes]
    return pl.pallas_call(
        kernel,
        out_shape=[jax.ShapeDtypeStruct(shape, kind) for shape, kind in out_shapes],
        in_specs=specs,
        out_specs=out_specs,
        scratch_shapes=list(scratch),
        compiler_params=pltpu.CompilerParams(vmem_limit_bytes=VMEM_LIMIT),
        cost_estimate=pl.CostEstimate(flops=flops, bytes_accessed=moved, transcendentals=0),
    )(*operands)


def payload_kernel(screen_ref, orbital_ref, out_ref, home_ref, held_ref, sems):
    first = pltpu.make_async_copy(screen_ref, held_ref, sems.at[0])
    second = pltpu.make_async_copy(orbital_ref, home_ref, sems.at[1])
    first.start()
    second.start()
    first.wait()
    pieces = []
    for q in range(2):
        for j in range(3):
            pieces.append(held_ref[q : q + 1, 256 * j : 256 * (j + 1)])
    rows = jnp.concatenate(pieces + [jnp.zeros((2, 256), F32)], axis=0)
    high = rows.astype(BF16)
    low = (rows - high.astype(F32)).astype(BF16)
    block = jnp.concatenate([high.astype(F32), low.astype(F32)], axis=0).astype(BF16)
    for target in range(16):
        out_ref[target] = block
    second.wait()


def pair_products(home_ref, far_ref, kind, out_ref):
    for a in range(2):
        top = a * 16 + kind * 8
        home_r = home_ref[top : top + 8, :].astype(F32)[:, None, :]
        home_i = home_ref[32 + top : 40 + top, :].astype(F32)[:, None, :]
        for b in range(2):
            top = b * 16 + kind * 8
            far_r = far_ref[top : top + 8, :].astype(F32)[None]
            far_i = far_ref[32 + top : 40 + top, :].astype(F32)[None]
            real = (home_r * far_r + home_i * far_i).reshape(64, 256).astype(BF16)
            imag = (home_r * far_i - home_i * far_r).reshape(64, 256).astype(BF16)
            at = (a * 2 + b) * 128
            out_ref[at : at + 64, 0:256] = real
            out_ref[at : at + 64, 256:512] = -imag
            out_ref[at + 64 : at + 128, 0:256] = imag
            out_ref[at + 64 : at + 128, 256:512] = real


def density_rows(pair_ref, fit_ref, out_ref):
    for half in range(2):
        at = half * 256
        out_ref[at : at + 256, :] = jnp.dot(
            pair_ref[at : at + 256, :], fit_ref[...], preferred_element_type=F32
        ).astype(BF16)


def fit_copies(fit_hbm_ref, fit_ref, sems):
    return [
        pltpu.make_async_copy(
            fit_hbm_ref.at[128 * i : 128 * (i + 1)], fit_ref.at[128 * i : 128 * (i + 1)], sems.at[i]
        )
        for i in range(4)
    ]


def density_kernel(home_ref, far2_ref, far3_ref, fit_hbm_ref, out_ref, fit_ref, pair_ref, sems):
    copies = fit_copies(fit_hbm_ref, fit_ref, sems)
    for copy in copies:
        copy.start()
    for index, far_ref in enumerate((far2_ref, far3_ref)):
        for kind in range(2):
            pair_products(home_ref, far_ref, kind, pair_ref.at[index, kind])
    for copy in copies:
        copy.wait()
    for index in range(2):
        for kind in range(2):
            density_rows(pair_ref.at[index, kind], fit_ref, out_ref.at[index, kind])


def blocks_of(step, table_ref, screen_ref, val_ref, cond_ref, weight_ref, out_ref):
    first_half = lax.broadcasted_iota(jnp.int32, (64, 128), 1) < 64
    rows = screen_ref[step + 1].astype(F32)
    rows = rows[0:8] + rows[8:16]
    stored = [
        jnp.concatenate([rows[3 * q + j : 3 * q + j + 1] for j in range(3)], axis=1) for q in range(2)
    ]
    for a in range(2):
        blocks = []
        for b in range(2):
            screen = jnp.where(table_ref[a, b] == 0, stored[0], stored[1])
            at = (a * 2 + b) * 128
            weight_ref[at : at + 128, :] = (val_ref[at : at + 128, :].astype(F32) * screen).astype(BF16)
            products = lax.dot_general(
                cond_ref[at : at + 128, :], weight_ref[at : at + 128, :], (((1,), (1,)), ((), ())),
                preferred_element_type=F32,
            )
            below = pltpu.roll(products[64:128], 64, 1)
            block = products[0:64] + jnp.where(first_half, below, -below)
            blocks.append(block.reshape(8, 8, 128))
        both = jnp.concatenate(blocks, axis=1).astype(BF16)
        for c in range(8):
            out_ref[a * 8 + c, step * 16 : (step + 1) * 16, :] = both[c]


def block_kernel(
    table_ref, home_ref, far1_ref, fit_hbm_ref, density_ref, screen_ref, out_ref,
    fit_ref, pair_ref, last_ref, weight_ref, sems,
):
    copies = fit_copies(fit_hbm_ref, fit_ref, sems)
    for copy in copies:
        copy.start()
    for kind in range(2):
        pair_products(home_ref, far1_ref, kind, pair_ref.at[kind])
    for index in range(2):
        blocks_of(
            index + 1, table_ref, screen_ref, density_ref.at[index, 0], density_ref.at[index, 1],
            weight_ref.at[index], out_ref,
        )
    for copy in copies:
        copy.wait()
    for kind in range(2):
        density_rows(pair_ref.at[kind], fit_ref, last_ref.at[kind])
    blocks_of(0, table_ref, screen_ref, last_ref.at[0], last_ref.at[1], weight_ref.at[2], out_ref)


def final_kernel(in_ref, out_ref):
    sublane = lax.broadcasted_iota(jnp.int32, (8, 128), 0)
    lane = lax.broadcasted_iota(jnp.int32, (8, 128), 1) // 8
    for step in range(STEPS):
        total = in_ref[0, step * 16 : (step + 1) * 16, :].astype(F32)
        for source in range(1, 16):
            total = total + in_ref[source, step * 16 : (step + 1) * 16, :].astype(F32)
        sides = []
        for b in range(2):
            x = total[b * 8 : (b + 1) * 8]
            for k in range(3):
                bit = 1 << k
                low = (sublane & bit) == 0
                low_lane = (lane & bit) == 0
                from_below = pltpu.roll(pltpu.roll(x, 8 - bit, 0), 8 * bit, 1)
                from_above = pltpu.roll(pltpu.roll(x, bit, 0), 128 - 8 * bit, 1)
                x = jnp.where(low == low_lane, x, jnp.where(low, from_below, from_above))
            sides.append(x)
        first_half = lane < 8
        out_ref[0, step] = jnp.where(first_half, sides[0], pltpu.roll(sides[1], 64, 1))
        out_ref[1, step] = jnp.where(first_half, pltpu.roll(sides[0], 64, 1), sides[1])


def body(orbitals, fit_vectors, screening, qpoint_table):
    vmem, smem = pltpu.VMEM, pltpu.SMEM
    width = fit_vectors.shape[2]

    def shifted(x, by, sources=range(16)):
        return lax.ppermute(x, "ka", [(i, (i + by) % 16) for i in sources])

    hbm = pltpu.HBM
    orbitals = orbitals.reshape(64, 256)
    far3, far2 = shifted(orbitals, 3), shifted(orbitals, 2)
    fit, given, screen = [
        pltpu.with_memory_space_constraint(x, hbm)
        for x in (fit_vectors.reshape(512, width), orbitals, screening[0])
    ]
    payload, home = call(
        payload_kernel, [((16, 16, 256), BF16), ((64, 256), BF16)], (screen, given), (hbm, hbm),
        [pltpu.VMEM((2, width), F32), pltpu.SemaphoreType.DMA((2,))], moved=200_000,
    )
    screens = lax.all_to_all(payload, "ka", 0, 0)
    far1 = shifted(home, 1)
    fit_scratch, fit_sems = pltpu.VMEM((512, width), BF16), pltpu.SemaphoreType.DMA((4,))
    (density,) = call(
        density_kernel,
        [((2, 2, 512, width), BF16)],
        (home, far2, far3, fit), (vmem, vmem, vmem, hbm),
        [fit_scratch, pltpu.VMEM((2, 2, 512, 512), BF16), fit_sems],
        flops=2 * 2 * 8 * 256 * 256 * width, moved=3_000_000,
    )
    (parts,) = call(
        block_kernel,
        [((16, 48, 128), BF16)],
        (qpoint_table, home, far1, fit, density, screens),
        (smem, vmem, vmem, hbm, vmem, vmem),
        [
            fit_scratch, pltpu.VMEM((2, 512, 512), BF16), pltpu.VMEM((2, 512, width), BF16),
            pltpu.VMEM((STEPS, 512, width), BF16), fit_sems,
        ],
        flops=2 * (8 * 256 * 256 + STEPS * 4 * 4 * 64 * 64) * width,
        moved=3_000_000,
    )
    parts = lax.all_to_all(parts, "ga", 0, 0)
    (out,) = call(final_kernel, [((2, STEPS, 8, 128), F32)], (parts,), (vmem,))
    return out[:, :, None]


def solution(mesh):
    in_specs = (P(None, "ka", None, None, None), P(None, None, "ga"), P("ka", None, "ga"), P())
    out_specs = P(None, None, "ka", "ga", None)
    return jax.shard_map(body, mesh=mesh, in_specs=in_specs, out_specs=out_specs, check_vma=False)
```

```python
import jax
import jax.numpy as jnp
from jax import lax
from jax.experimental import pallas as pl
from jax.experimental.pallas import tpu as pltpu
from jax.sharding import PartitionSpec as P

NV = 8
STEPS = 3
BF16 = jnp.bfloat16
F32 = jnp.float32
VMEM_LIMIT = 24 * 1024 * 1024


def call(kernel, out_shapes, operands, spaces, scratch=(), flops=0, moved=0):
    specs = [pl.BlockSpec(memory_space=space) for space in spaces]
    out_specs = [pl.BlockSpec(memory_space=pltpu.VMEM) for _ in out_shapes]
    return pl.pallas_call(
        kernel,
        out_shape=[jax.ShapeDtypeStruct(shape, kind) for shape, kind in out_shapes],
        in_specs=specs,
        out_specs=out_specs,
        scratch_shapes=list(scratch),
        compiler_params=pltpu.CompilerParams(vmem_limit_bytes=VMEM_LIMIT),
        cost_estimate=pl.CostEstimate(flops=flops, bytes_accessed=moved, transcendentals=0),
    )(*operands)


def payload_kernel(screen_ref, orbital_ref, out_ref, home_ref, held_ref, sems):
    first = pltpu.make_async_copy(screen_ref, held_ref, sems.at[0])
    second = pltpu.make_async_copy(orbital_ref, home_ref, sems.at[1])
    first.start()
    second.start()
    first.wait()
    pieces = []
    for q in range(2):
        for j in range(3):
            pieces.append(held_ref[q : q + 1, 256 * j : 256 * (j + 1)])
    rows = jnp.concatenate(pieces + [jnp.zeros((2, 256), F32)], axis=0)
    high = rows.astype(BF16)
    low = (rows - high.astype(F32)).astype(BF16)
    block = jnp.concatenate([high.astype(F32), low.astype(F32)], axis=0).astype(BF16)
    for target in range(16):
        out_ref[target] = block
    second.wait()


def pair_products(home_ref, far_ref, kind, out_ref):
    for a in range(2):
        top = a * 16 + kind * 8
        home_r = home_ref[top : top + 8, :].astype(F32)[:, None, :]
        home_i = home_ref[32 + top : 40 + top, :].astype(F32)[:, None, :]
        for b in range(2):
            top = b * 16 + kind * 8
            far_r = far_ref[top : top + 8, :].astype(F32)[None]
            far_i = far_ref[32 + top : 40 + top, :].astype(F32)[None]
            real = (home_r * far_r + home_i * far_i).reshape(64, 256).astype(BF16)
            imag = (home_r * far_i - home_i * far_r).reshape(64, 256).astype(BF16)
            at = (a * 2 + b) * 128
            out_ref[at : at + 64, 0:256] = real
            out_ref[at : at + 64, 256:512] = -imag
            out_ref[at + 64 : at + 128, 0:256] = imag
            out_ref[at + 64 : at + 128, 256:512] = real


def density_rows(pair_ref, fit_ref, out_ref):
    for half in range(2):
        at = half * 256
        out_ref[at : at + 256, :] = jnp.dot(
            pair_ref[at : at + 256, :], fit_ref[...], preferred_element_type=F32
        ).astype(BF16)


def fit_copies(fit_hbm_ref, fit_ref, sems):
    return [
        pltpu.make_async_copy(
            fit_hbm_ref.at[128 * i : 128 * (i + 1)], fit_ref.at[128 * i : 128 * (i + 1)], sems.at[i]
        )
        for i in range(4)
    ]


def density_kernel(home_ref, far2_ref, far3_ref, fit_hbm_ref, out_ref, fit_ref, pair_ref, sems):
    copies = fit_copies(fit_hbm_ref, fit_ref, sems)
    for copy in copies:
        copy.start()
    for index, far_ref in enumerate((far2_ref, far3_ref)):
        for kind in range(2):
            pair_products(home_ref, far_ref, kind, pair_ref.at[index, kind])
    for copy in copies:
        copy.wait()
    for index in range(2):
        for kind in range(2):
            density_rows(pair_ref.at[index, kind], fit_ref, out_ref.at[index, kind])


def blocks_of(slot, step, table_ref, screen_ref, val_ref, cond_ref, weight_ref, out_ref):
    first_half = lax.broadcasted_iota(jnp.int32, (64, 128), 1) < 64
    rows = screen_ref[step + 1].astype(F32)
    rows = rows[0:8] + rows[8:16]
    stored = [
        jnp.concatenate([rows[3 * q + j : 3 * q + j + 1] for j in range(3)], axis=1) for q in range(2)
    ]
    for a in range(2):
        blocks = []
        for b in range(2):
            screen = jnp.where(table_ref[a, b] == 0, stored[0], stored[1])
            at = (a * 2 + b) * 128
            weight_ref[at : at + 128, :] = (val_ref[at : at + 128, :].astype(F32) * screen).astype(BF16)
            products = lax.dot_general(
                cond_ref[at : at + 128, :], weight_ref[at : at + 128, :], (((1,), (1,)), ((), ())),
                preferred_element_type=F32,
            )
            below = pltpu.roll(products[64:128], 64, 1)
            block = products[0:64] + jnp.where(first_half, below, -below)
            blocks.append(block.reshape(8, 8, 128))
        both = jnp.concatenate(blocks, axis=1).astype(BF16)
        for c in range(8):
            out_ref[a * 8 + c, slot * 16 : (slot + 1) * 16, :] = both[c]


def early_kernel(table_ref, fit_hbm_ref, density_ref, screen_ref, out_ref, fit_ref, weight_ref, sems):
    copies = fit_copies(fit_hbm_ref, fit_ref, sems)
    for copy in copies:
        copy.start()
    for index in range(2):
        blocks_of(
            index, index + 1, table_ref, screen_ref, density_ref.at[index, 0], density_ref.at[index, 1],
            weight_ref.at[index], out_ref,
        )
    for copy in copies:
        copy.wait()


def late_kernel(table_ref, home_ref, far_ref, fit_ref, screen_ref, early_ref, out_ref, pair_ref, density_ref, weight_ref):
    for kind in range(2):
        pair_products(home_ref, far_ref, kind, pair_ref.at[kind])
        density_rows(pair_ref.at[kind], fit_ref, density_ref.at[kind])
    out_ref[:, 16:48, :] = early_ref[...]
    blocks_of(0, 0, table_ref, screen_ref, density_ref.at[0], density_ref.at[1], weight_ref, out_ref)


def final_kernel(in_ref, out_ref):
    sublane = lax.broadcasted_iota(jnp.int32, (8, 128), 0)
    lane = lax.broadcasted_iota(jnp.int32, (8, 128), 1) // 8
    for step in range(STEPS):
        total = in_ref[0, step * 16 : (step + 1) * 16, :].astype(F32)
        for source in range(1, 16):
            total = total + in_ref[source, step * 16 : (step + 1) * 16, :].astype(F32)
        sides = []
        for b in range(2):
            x = total[b * 8 : (b + 1) * 8]
            for k in range(3):
                bit = 1 << k
                low = (sublane & bit) == 0
                low_lane = (lane & bit) == 0
                from_below = pltpu.roll(pltpu.roll(x, 8 - bit, 0), 8 * bit, 1)
                from_above = pltpu.roll(pltpu.roll(x, bit, 0), 128 - 8 * bit, 1)
                x = jnp.where(low == low_lane, x, jnp.where(low, from_below, from_above))
            sides.append(x)
        first_half = lane < 8
        out_ref[0, step] = jnp.where(first_half, sides[0], pltpu.roll(sides[1], 64, 1))
        out_ref[1, step] = jnp.where(first_half, pltpu.roll(sides[0], 64, 1), sides[1])


def body(orbitals, fit_vectors, screening, qpoint_table):
    vmem, smem = pltpu.VMEM, pltpu.SMEM
    width = fit_vectors.shape[2]

    def shifted(x, by, sources=range(16)):
        return lax.ppermute(x, "ka", [(i, (i + by) % 16) for i in sources])

    hbm = pltpu.HBM
    orbitals = orbitals.reshape(64, 256)
    far3, far2 = shifted(orbitals, 3), shifted(orbitals, 2)
    fit, given, screen = [
        pltpu.with_memory_space_constraint(x, hbm)
        for x in (fit_vectors.reshape(512, width), orbitals, screening[0])
    ]
    payload, home = call(
        payload_kernel, [((16, 16, 256), BF16), ((64, 256), BF16)], (screen, given), (hbm, hbm),
        [pltpu.VMEM((2, width), F32), pltpu.SemaphoreType.DMA((2,))], moved=200_000,
    )
    screens = lax.all_to_all(payload, "ka", 0, 0)
    far1 = shifted(home, 1)
    fit_scratch, fit_sems = pltpu.VMEM((512, width), BF16), pltpu.SemaphoreType.DMA((4,))
    (density,) = call(
        density_kernel,
        [((2, 2, 512, width), BF16)],
        (home, far2, far3, fit), (vmem, vmem, vmem, hbm),
        [fit_scratch, pltpu.VMEM((2, 2, 512, 512), BF16), fit_sems],
        flops=2 * 2 * 8 * 256 * 256 * width, moved=3_000_000,
    )
    early, fit = call(
        early_kernel,
        [((16, 32, 128), BF16), ((512, width), BF16)],
        (qpoint_table, fit, density, screens), (smem, hbm, vmem, vmem),
        [pltpu.VMEM((2, 512, width), BF16), fit_sems],
        flops=2 * 2 * 4 * 4 * 64 * 64 * width, moved=3_000_000,
    )
    (parts,) = call(
        late_kernel,
        [((16, 48, 128), BF16)],
        (qpoint_table, home, far1, fit, screens, early),
        (smem,) + (vmem,) * 5,
        [pltpu.VMEM((2, 512, 512), BF16), pltpu.VMEM((2, 512, width), BF16), pltpu.VMEM((512, width), BF16)],
        flops=2 * (8 * 256 * 256 + 4 * 4 * 64 * 64) * width,
        moved=2_000_000,
    )
    parts = lax.all_to_all(parts, "ga", 0, 0)
    (out,) = call(final_kernel, [((2, STEPS, 8, 128), F32)], (parts,), (vmem,))
    return out[:, :, None]


def solution(mesh):
    in_specs = (P(None, "ka", None, None, None), P(None, None, "ga"), P("ka", None, "ga"), P())
    out_specs = P(None, None, "ka", "ga", None)
    return jax.shard_map(body, mesh=mesh, in_specs=in_specs, out_specs=out_specs, check_vma=False)
```

```python
import jax
import jax.numpy as jnp
from jax import lax
from jax.experimental import pallas as pl
from jax.experimental.pallas import tpu as pltpu
from jax.sharding import PartitionSpec as P

NV = 8
STEPS = 3
BF16 = jnp.bfloat16
F32 = jnp.float32
VMEM_LIMIT = 24 * 1024 * 1024


def call(kernel, out_shapes, operands, spaces, scratch=(), flops=0, moved=0):
    specs = [pl.BlockSpec(memory_space=space) for space in spaces]
    out_specs = [pl.BlockSpec(memory_space=pltpu.VMEM) for _ in out_shapes]
    return pl.pallas_call(
        kernel,
        out_shape=[jax.ShapeDtypeStruct(shape, kind) for shape, kind in out_shapes],
        in_specs=specs,
        out_specs=out_specs,
        scratch_shapes=list(scratch),
        compiler_params=pltpu.CompilerParams(vmem_limit_bytes=VMEM_LIMIT),
        cost_estimate=pl.CostEstimate(flops=flops, bytes_accessed=moved, transcendentals=0),
    )(*operands)


def row_kernel(own_ref, in1_ref, in2_ref, in3_ref, out_ref):
    out_ref[...] = jnp.where(lax.axis_index("ka") < 4, own_ref[...], in1_ref[...] + in2_ref[...] + in3_ref[...])


def copy_kernel(row_ref, landed_ref, out_ref):
    out_ref[...] = row_ref[...]


def fetch_kernel(*refs):
    count = len(refs) // 2
    copies = [pltpu.make_async_copy(refs[i], refs[count + i], refs[-1].at[i]) for i in range(count)]
    for copy in copies:
        copy.start()
    for copy in copies:
        copy.wait()


def pair_products(home_ref, far_ref, kind, out_ref):
    for a in range(2):
        top = a * 16 + kind * 8
        home_r = home_ref[top : top + 8, :].astype(F32)[:, None, :]
        home_i = home_ref[32 + top : 40 + top, :].astype(F32)[:, None, :]
        for b in range(2):
            top = b * 16 + kind * 8
            far_r = far_ref[top : top + 8, :].astype(F32)[None]
            far_i = far_ref[32 + top : 40 + top, :].astype(F32)[None]
            real = (home_r * far_r + home_i * far_i).reshape(64, 256).astype(BF16)
            imag = (home_r * far_i - home_i * far_r).reshape(64, 256).astype(BF16)
            at = (a * 2 + b) * 128
            out_ref[at : at + 64, 0:256] = real
            out_ref[at : at + 64, 256:512] = -imag
            out_ref[at + 64 : at + 128, 0:256] = imag
            out_ref[at + 64 : at + 128, 256:512] = real


def density_rows(pair_ref, fit_ref, out_ref):
    for half in range(2):
        at = half * 256
        out_ref[at : at + 256, :] = jnp.dot(
            pair_ref[at : at + 256, :], fit_ref[...], preferred_element_type=F32
        ).astype(BF16)


def density_kernel(home_ref, far1_ref, far2_ref, far3_ref, fit_ref, out_ref, pair_ref):
    for step, far_ref in enumerate((far1_ref, far2_ref, far3_ref)):
        for kind in range(2):
            pair_products(home_ref, far_ref, kind, pair_ref.at[step, kind])
            density_rows(pair_ref.at[step, kind], fit_ref, out_ref.at[step, kind])


def blocks_of(step, table_ref, stored, val_ref, cond_ref, weight_ref, out_ref):
    first_half = lax.broadcasted_iota(jnp.int32, (64, 128), 1) < 64
    for a in range(2):
        blocks = []
        for b in range(2):
            screen = jnp.where(table_ref[a, b] == 0, stored[0], stored[1])
            at = (a * 2 + b) * 128
            weight_ref[at : at + 128, :] = (val_ref[at : at + 128, :].astype(F32) * screen).astype(BF16)
            products = lax.dot_general(
                cond_ref[at : at + 128, :], weight_ref[at : at + 128, :], (((1,), (1,)), ((), ())),
                preferred_element_type=F32,
            )
            below = pltpu.roll(products[64:128], 64, 1)
            block = products[0:64] + jnp.where(first_half, below, -below)
            blocks.append(block.reshape(8, 8, 128))
        both = jnp.concatenate(blocks, axis=1).astype(BF16)
        for c in range(8):
            out_ref[a * 8 + c, step * 16 : (step + 1) * 16, :] = both[c]


def mixing_kernel(table_ref, row0_ref, row1_ref, row2_ref, row3_ref, density_ref, out_ref, weight_ref):
    place = lax.rem(lax.axis_index("ka"), 4)
    sent = [ref[...] for ref in (row0_ref, row1_ref, row2_ref, row3_ref)]
    for step in range(STEPS):
        away = place ^ (step + 1)
        rows = jnp.where(away == 0, sent[0], jnp.where(away == 1, sent[1], jnp.where(away == 2, sent[2], sent[3])))
        blocks_of(
            step, table_ref, [rows[0:1], rows[1:2]], density_ref.at[step, 0], density_ref.at[step, 1],
            weight_ref.at[step], out_ref,
        )


def final_kernel(in_ref, out_ref):
    sublane = lax.broadcasted_iota(jnp.int32, (8, 128), 0)
    lane = lax.broadcasted_iota(jnp.int32, (8, 128), 1) // 8
    for step in range(STEPS):
        total = in_ref[0, step * 16 : (step + 1) * 16, :].astype(F32)
        for source in range(1, 16):
            total = total + in_ref[source, step * 16 : (step + 1) * 16, :].astype(F32)
        sides = []
        for b in range(2):
            x = total[b * 8 : (b + 1) * 8]
            for k in range(3):
                bit = 1 << k
                low = (sublane & bit) == 0
                low_lane = (lane & bit) == 0
                from_below = pltpu.roll(pltpu.roll(x, 8 - bit, 0), 8 * bit, 1)
                from_above = pltpu.roll(pltpu.roll(x, bit, 0), 128 - 8 * bit, 1)
                x = jnp.where(low == low_lane, x, jnp.where(low, from_below, from_above))
            sides.append(x)
        first_half = lane < 8
        out_ref[0, step] = jnp.where(first_half, sides[0], pltpu.roll(sides[1], 64, 1))
        out_ref[1, step] = jnp.where(first_half, pltpu.roll(sides[0], 64, 1), sides[1])


def body(orbitals, fit_vectors, screening, qpoint_table):
    vmem, smem = pltpu.VMEM, pltpu.SMEM
    width = fit_vectors.shape[2]

    def shifted(x, by, sources=range(16)):
        return lax.ppermute(x, "ka", [(i, (i + by) % 16) for i in sources])

    hbm = pltpu.HBM
    orbitals = orbitals.reshape(64, 256)
    far = [shifted(orbitals, by) for by in range(1, STEPS + 1)]
    given = (fit_vectors.reshape(512, width), orbitals, screening[0])
    fit, home, screen = call(
        fetch_kernel, [(x.shape, x.dtype) for x in given],
        [pltpu.with_memory_space_constraint(x, hbm) for x in given],
        (hbm,) * 3, [pltpu.SemaphoreType.DMA((3,))], moved=1_700_000,
    )
    (again,) = call(copy_kernel, [((2, width), F32)], (screen, far[2]), (vmem, pl.ANY))
    come = [shifted(x, by, range(1, STEPS + 1)) for x, by in ((again, 4), (screen, 8), (screen, 12))]
    (row,) = call(row_kernel, [((2, width), F32)], (screen, *come), (vmem,) * 4)
    rows = [row] + [lax.ppermute(row, "ka", [(i, i ^ mask) for i in range(16)]) for mask in (1, 2, 3)]
    (density,) = call(
        density_kernel, [((STEPS, 2, 512, width), BF16)], (home, *far, fit), (vmem,) * 5,
        [pltpu.VMEM((STEPS, 2, 512, 512), BF16)], flops=2 * STEPS * 8 * 256 * 256 * width, moved=6_000_000,
    )
    (parts,) = call(
        mixing_kernel, [((16, 48, 128), BF16)], (qpoint_table, *rows, density), (smem,) + (vmem,) * 5,
        [pltpu.VMEM((STEPS, 512, width), BF16)],
        flops=2 * STEPS * 4 * 4 * 64 * 64 * width, moved=6_000_000,
    )
    parts = lax.all_to_all(parts, "ga", 0, 0)
    (out,) = call(final_kernel, [((2, STEPS, 8, 128), F32)], (parts,), (vmem,))
    return out[:, :, None]


def solution(mesh):
    in_specs = (P(None, "ka", None, None, None), P(None, None, "ga"), P("ka", None, "ga"), P())
    out_specs = P(None, None, "ka", "ga", None)
    return jax.shard_map(body, mesh=mesh, in_specs=in_specs, out_specs=out_specs, check_vma=False)
```

```python
import jax
import jax.numpy as jnp
from jax import lax
from jax.experimental import pallas as pl
from jax.experimental.pallas import tpu as pltpu
from jax.sharding import PartitionSpec as P

NV = 8
STEPS = 3
GA_ORDER = [8 * half + z for z in (0, 3, 6, 1, 4, 7, 2, 5) for half in range(2)]
KA_ORDER = list(range(15, -1, -1))
BF16 = jnp.bfloat16
F32 = jnp.float32
VMEM_LIMIT = 24 * 1024 * 1024


def call(kernel, out_shapes, operands, spaces, scratch=(), flops=0, moved=0):
    specs = [pl.BlockSpec(memory_space=space) for space in spaces]
    out_specs = [pl.BlockSpec(memory_space=pltpu.VMEM) for _ in out_shapes]
    return pl.pallas_call(
        kernel,
        out_shape=[jax.ShapeDtypeStruct(shape, kind) for shape, kind in out_shapes],
        in_specs=specs,
        out_specs=out_specs,
        scratch_shapes=list(scratch),
        compiler_params=pltpu.CompilerParams(vmem_limit_bytes=VMEM_LIMIT),
        cost_estimate=pl.CostEstimate(flops=flops, bytes_accessed=moved, transcendentals=0),
    )(*operands)


def payload_kernel(screen_ref, out_ref, held_ref, sem):
    copy = pltpu.make_async_copy(screen_ref, held_ref, sem)
    copy.start()
    copy.wait()
    pieces = []
    for q in range(2):
        for j in range(3):
            pieces.append(held_ref[q : q + 1, 256 * j : 256 * (j + 1)])
    rows = jnp.concatenate(pieces + [jnp.zeros((2, 256), F32)], axis=0)
    high = rows.astype(BF16)
    low = (rows - high.astype(F32)).astype(BF16)
    block = jnp.concatenate([high.astype(F32), low.astype(F32)], axis=0).astype(BF16)
    for target in range(16):
        out_ref[target] = block


def pair_products(home_ref, far_ref, kind, out_ref):
    for a in range(2):
        top = a * 16 + kind * 8
        home_r = home_ref[top : top + 8, :].astype(F32)[:, None, :]
        home_i = home_ref[32 + top : 40 + top, :].astype(F32)[:, None, :]
        for b in range(2):
            top = b * 16 + kind * 8
            far_r = far_ref[top : top + 8, :].astype(F32)[None]
            far_i = far_ref[32 + top : 40 + top, :].astype(F32)[None]
            real = (home_r * far_r + home_i * far_i).reshape(64, 256).astype(BF16)
            imag = (home_r * far_i - home_i * far_r).reshape(64, 256).astype(BF16)
            at = (a * 2 + b) * 128
            out_ref[at : at + 64, 0:256] = real
            out_ref[at : at + 64, 256:512] = -imag
            out_ref[at + 64 : at + 128, 0:256] = imag
            out_ref[at + 64 : at + 128, 256:512] = real


def density_rows(pair_ref, fit_ref, out_ref):
    for half in range(2):
        at = half * 256
        out_ref[at : at + 256, :] = jnp.dot(
            pair_ref[at : at + 256, :], fit_ref[...], preferred_element_type=F32
        ).astype(BF16)


def valence_kernel(
    orbital_ref, far1_ref, far2_ref, far3_ref, fit_hbm_ref, home_ref, fit_ref, val_ref, pair_ref, sems
):
    home_copy = pltpu.make_async_copy(orbital_ref, home_ref, sems.at[0])
    fit_copy = pltpu.make_async_copy(fit_hbm_ref, fit_ref, sems.at[1])
    home_copy.start()
    fit_copy.start()
    home_copy.wait()
    for step, far_ref in enumerate((far1_ref, far2_ref, far3_ref)):
        pair_products(home_ref, far_ref, 0, pair_ref.at[step])
    fit_copy.wait()
    for step in range(STEPS):
        density_rows(pair_ref.at[step], fit_ref, val_ref.at[step])


def block_kernel(
    table_ref, home_ref, far1_ref, far2_ref, far3_ref, fit_ref, val_ref, screen_ref, out_ref,
    pair_ref, cond_ref, weight_ref,
):
    first_half = lax.broadcasted_iota(jnp.int32, (64, 128), 1) < 64
    for step, far_ref in enumerate((far1_ref, far2_ref, far3_ref)):
        pair_products(home_ref, far_ref, 1, pair_ref.at[step])
        rows = screen_ref[KA_ORDER.index(step + 1)].astype(F32)
        rows = rows[0:8] + rows[8:16]
        stored = [
            jnp.concatenate([rows[3 * q + j : 3 * q + j + 1] for j in range(3)], axis=1) for q in range(2)
        ]
        for a in range(2):
            for b in range(2):
                screen = jnp.where(table_ref[a, b] == 0, stored[0], stored[1])
                at = (a * 2 + b) * 128
                weight_ref[step, at : at + 128, :] = (val_ref[step, at : at + 128, :].astype(F32) * screen).astype(BF16)
        density_rows(pair_ref.at[step], fit_ref, cond_ref.at[step])
        for a in range(2):
            blocks = []
            for b in range(2):
                at = (a * 2 + b) * 128
                products = lax.dot_general(
                    cond_ref[step, at : at + 128, :], weight_ref[step, at : at + 128, :], (((1,), (1,)), ((), ())),
                    preferred_element_type=F32,
                )
                below = pltpu.roll(products[64:128], 64, 1)
                block = products[0:64] + jnp.where(first_half, below, -below)
                blocks.append(block.reshape(8, 8, 128))
            both = jnp.concatenate(blocks, axis=1).astype(BF16)
            for c in range(8):
                out_ref[GA_ORDER.index(a * 8 + c), step * 16 : (step + 1) * 16, :] = both[c]


def final_kernel(in_ref, out_ref):
    sublane = lax.broadcasted_iota(jnp.int32, (8, 128), 0)
    lane = lax.broadcasted_iota(jnp.int32, (8, 128), 1) // 8
    for step in range(STEPS):
        total = in_ref[0, step * 16 : (step + 1) * 16, :].astype(F32)
        for source in range(1, 16):
            total = total + in_ref[source, step * 16 : (step + 1) * 16, :].astype(F32)
        sides = []
        for b in range(2):
            x = total[b * 8 : (b + 1) * 8]
            for k in range(3):
                bit = 1 << k
                low = (sublane & bit) == 0
                low_lane = (lane & bit) == 0
                from_below = pltpu.roll(pltpu.roll(x, 8 - bit, 0), 8 * bit, 1)
                from_above = pltpu.roll(pltpu.roll(x, bit, 0), 128 - 8 * bit, 1)
                x = jnp.where(low == low_lane, x, jnp.where(low, from_below, from_above))
            sides.append(x)
        first_half = lane < 8
        out_ref[0, step] = jnp.where(first_half, sides[0], pltpu.roll(sides[1], 64, 1))
        out_ref[1, step] = jnp.where(first_half, pltpu.roll(sides[0], 64, 1), sides[1])


def body(orbitals, fit_vectors, screening, qpoint_table):
    vmem, smem = pltpu.VMEM, pltpu.SMEM
    width = fit_vectors.shape[2]

    def shifted(x, by, sources=range(16)):
        return lax.ppermute(x, "ka", [(i, (i + by) % 16) for i in sources])

    hbm = pltpu.HBM
    orbitals = orbitals.reshape(64, 256)
    far = [shifted(orbitals, by) for by in range(1, STEPS + 1)]
    fit, home, screen = [
        pltpu.with_memory_space_constraint(x, hbm)
        for x in (fit_vectors.reshape(512, width), orbitals, screening[0])
    ]
    (payload,) = call(
        payload_kernel, [((16, 16, 256), BF16)], (screen,), (hbm,),
        [pltpu.VMEM((2, width), F32), pltpu.SemaphoreType.DMA], moved=200_000,
    )
    screens = lax.all_to_all(payload, "ka", 0, 0, axis_index_groups=[KA_ORDER])
    home, fit, val = call(
        valence_kernel,
        [((64, 256), BF16), ((512, width), BF16), ((STEPS, 512, width), BF16)],
        (home, *far, fit), (hbm, vmem, vmem, vmem, hbm),
        [pltpu.VMEM((STEPS, 512, 512), BF16), pltpu.SemaphoreType.DMA((2,))],
        flops=2 * STEPS * 4 * 256 * 256 * width, moved=3_000_000,
    )
    (parts,) = call(
        block_kernel,
        [((16, 48, 128), BF16)],
        (qpoint_table, home, *far, fit, val, screens),
        (smem,) + (vmem,) * 7,
        [
            pltpu.VMEM((STEPS, 512, 512), BF16), pltpu.VMEM((STEPS, 512, width), BF16),
            pltpu.VMEM((STEPS, 512, width), BF16),
        ],
        flops=2 * STEPS * (4 * 256 * 256 + 4 * 4 * 64 * 64) * width,
        moved=3_000_000,
    )
    parts = lax.all_to_all(parts, "ga", 0, 0, axis_index_groups=[GA_ORDER])
    (out,) = call(final_kernel, [((2, STEPS, 8, 128), F32)], (parts,), (vmem,))
    return out[:, :, None]


def solution(mesh):
    in_specs = (P(None, "ka", None, None, None), P(None, None, "ga"), P("ka", None, "ga"), P())
    out_specs = P(None, None, "ka", "ga", None)
    return jax.shard_map(body, mesh=mesh, in_specs=in_specs, out_specs=out_specs, check_vma=False)
```

```python
import jax
import jax.numpy as jnp
from jax import lax
from jax.experimental import pallas as pl
from jax.experimental.pallas import tpu as pltpu
from jax.sharding import PartitionSpec as P

NV = 8
STEPS = 3
GA_ORDER = [8 * half + z for z in (0, 3, 6, 1, 4, 7, 2, 5) for half in range(2)]
KA_ORDER = list(range(15, -1, -1))
BF16 = jnp.bfloat16
F32 = jnp.float32
VMEM_LIMIT = 24 * 1024 * 1024


def call(kernel, out_shapes, operands, spaces, scratch=(), flops=0, moved=0, in_hbm=()):
    specs = [pl.BlockSpec(memory_space=space) for space in spaces]
    out_specs = [
        pl.BlockSpec(memory_space=pltpu.HBM if index in in_hbm else pltpu.VMEM) for index in range(len(out_shapes))
    ]
    return pl.pallas_call(
        kernel,
        out_shape=[
            pltpu.HBM(shape, kind) if index in in_hbm else jax.ShapeDtypeStruct(shape, kind)
            for index, (shape, kind) in enumerate(out_shapes)
        ],
        in_specs=specs,
        out_specs=out_specs,
        scratch_shapes=list(scratch),
        compiler_params=pltpu.CompilerParams(vmem_limit_bytes=VMEM_LIMIT),
        cost_estimate=pl.CostEstimate(flops=flops, bytes_accessed=moved, transcendentals=0),
    )(*operands)


def payload_kernel(screen_ref, out_ref, held_ref, sem):
    copy = pltpu.make_async_copy(screen_ref, held_ref, sem)
    copy.start()
    copy.wait()
    pieces = []
    for q in range(2):
        for j in range(3):
            pieces.append(held_ref[q : q + 1, 256 * j : 256 * (j + 1)])
    rows = jnp.concatenate(pieces + [jnp.zeros((2, 256), F32)], axis=0)
    high = rows.astype(BF16)
    low = (rows - high.astype(F32)).astype(BF16)
    block = jnp.concatenate([high.astype(F32), low.astype(F32)], axis=0).astype(BF16)
    for target in range(16):
        out_ref[target] = block


def pair_products(home_ref, far_ref, kind, out_ref):
    for a in range(2):
        top = a * 16 + kind * 8
        home_r = home_ref[top : top + 8, :].astype(F32)[:, None, :]
        home_i = home_ref[32 + top : 40 + top, :].astype(F32)[:, None, :]
        for b in range(2):
            top = b * 16 + kind * 8
            far_r = far_ref[top : top + 8, :].astype(F32)[None]
            far_i = far_ref[32 + top : 40 + top, :].astype(F32)[None]
            real = (home_r * far_r + home_i * far_i).reshape(64, 256).astype(BF16)
            imag = (home_r * far_i - home_i * far_r).reshape(64, 256).astype(BF16)
            at = (a * 2 + b) * 128
            out_ref[at : at + 64, 0:256] = real
            out_ref[at : at + 64, 256:512] = -imag
            out_ref[at + 64 : at + 128, 0:256] = imag
            out_ref[at + 64 : at + 128, 256:512] = real


def density_rows(pair_ref, fit_ref, out_ref):
    for half in range(2):
        at = half * 256
        out_ref[at : at + 256, :] = jnp.dot(
            pair_ref[at : at + 256, :], fit_ref[...], preferred_element_type=F32
        ).astype(BF16)


def valence_kernel(
    orbital_ref, far1_ref, far2_ref, far3_ref, fit_hbm_ref, home_ref, fit_ref, val_ref, aside_ref,
    pair_ref, cond_ref, sems,
):
    home_copy = pltpu.make_async_copy(orbital_ref, home_ref, sems.at[0])
    fit_copy = pltpu.make_async_copy(fit_hbm_ref, fit_ref, sems.at[1])
    home_copy.start()
    fit_copy.start()
    home_copy.wait()
    pair_products(home_ref, far3_ref, 1, pair_ref.at[STEPS])
    for step, far_ref in enumerate((far1_ref, far2_ref, far3_ref)):
        pair_products(home_ref, far_ref, 0, pair_ref.at[step])
    fit_copy.wait()
    density_rows(pair_ref.at[STEPS], fit_ref, cond_ref)
    aside_copy = pltpu.make_async_copy(cond_ref, aside_ref, sems.at[2])
    aside_copy.start()
    for step in range(STEPS):
        density_rows(pair_ref.at[step], fit_ref, val_ref.at[step])
    aside_copy.wait()


def block_kernel(
    table_ref, home_ref, far1_ref, far2_ref, fit_ref, val_ref, aside_ref, screen_ref, out_ref,
    pair_ref, cond_ref, weight_ref, sem,
):
    aside_copy = pltpu.make_async_copy(aside_ref, cond_ref.at[2], sem)
    aside_copy.start()
    first_half = lax.broadcasted_iota(jnp.int32, (64, 128), 1) < 64
    for step, far_ref in enumerate((far1_ref, far2_ref, None)):
        if far_ref is not None:
            pair_products(home_ref, far_ref, 1, pair_ref.at[step])
        rows = screen_ref[KA_ORDER.index(step + 1)].astype(F32)
        rows = rows[0:8] + rows[8:16]
        stored = [
            jnp.concatenate([rows[3 * q + j : 3 * q + j + 1] for j in range(3)], axis=1) for q in range(2)
        ]
        for a in range(2):
            for b in range(2):
                screen = jnp.where(table_ref[a, b] == 0, stored[0], stored[1])
                at = (a * 2 + b) * 128
                weight_ref[step, at : at + 128, :] = (val_ref[step, at : at + 128, :].astype(F32) * screen).astype(BF16)
        if far_ref is not None:
            density_rows(pair_ref.at[step], fit_ref, cond_ref.at[step])
        else:
            aside_copy.wait()
        for a in range(2):
            blocks = []
            for b in range(2):
                at = (a * 2 + b) * 128
                products = lax.dot_general(
                    cond_ref[step, at : at + 128, :], weight_ref[step, at : at + 128, :], (((1,), (1,)), ((), ())),
                    preferred_element_type=F32,
                )
                below = pltpu.roll(products[64:128], 64, 1)
                block = products[0:64] + jnp.where(first_half, below, -below)
                blocks.append(block.reshape(8, 8, 128))
            both = jnp.concatenate(blocks, axis=1).astype(BF16)
            for c in range(8):
                out_ref[GA_ORDER.index(a * 8 + c), step * 16 : (step + 1) * 16, :] = both[c]


def final_kernel(in_ref, out_ref):
    sublane = lax.broadcasted_iota(jnp.int32, (8, 128), 0)
    lane = lax.broadcasted_iota(jnp.int32, (8, 128), 1) // 8
    for step in range(STEPS):
        total = in_ref[0, step * 16 : (step + 1) * 16, :].astype(F32)
        for source in range(1, 16):
            total = total + in_ref[source, step * 16 : (step + 1) * 16, :].astype(F32)
        sides = []
        for b in range(2):
            x = total[b * 8 : (b + 1) * 8]
            for k in range(3):
                bit = 1 << k
                low = (sublane & bit) == 0
                low_lane = (lane & bit) == 0
                from_below = pltpu.roll(pltpu.roll(x, 8 - bit, 0), 8 * bit, 1)
                from_above = pltpu.roll(pltpu.roll(x, bit, 0), 128 - 8 * bit, 1)
                x = jnp.where(low == low_lane, x, jnp.where(low, from_below, from_above))
            sides.append(x)
        first_half = lane < 8
        out_ref[0, step] = jnp.where(first_half, sides[0], pltpu.roll(sides[1], 64, 1))
        out_ref[1, step] = jnp.where(first_half, pltpu.roll(sides[0], 64, 1), sides[1])


def body(orbitals, fit_vectors, screening, qpoint_table):
    vmem, smem = pltpu.VMEM, pltpu.SMEM
    width = fit_vectors.shape[2]

    def shifted(x, by, sources=range(16)):
        return lax.ppermute(x, "ka", [(i, (i + by) % 16) for i in sources])

    hbm = pltpu.HBM
    orbitals = orbitals.reshape(64, 256)
    far = [shifted(orbitals, by) for by in range(1, STEPS + 1)]
    fit, home, screen = [
        pltpu.with_memory_space_constraint(x, hbm)
        for x in (fit_vectors.reshape(512, width), orbitals, screening[0])
    ]
    (payload,) = call(
        payload_kernel, [((16, 16, 256), BF16)], (screen,), (hbm,),
        [pltpu.VMEM((2, width), F32), pltpu.SemaphoreType.DMA], moved=200_000,
    )
    screens = lax.all_to_all(payload, "ka", 0, 0, axis_index_groups=[KA_ORDER])
    home, fit, val, aside = call(
        valence_kernel,
        [((64, 256), BF16), ((512, width), BF16), ((STEPS, 512, width), BF16), ((512, width), BF16)],
        (home, *far, fit), (hbm, vmem, vmem, vmem, hbm),
        [pltpu.VMEM((STEPS + 1, 512, 512), BF16), pltpu.VMEM((512, width), BF16), pltpu.SemaphoreType.DMA((3,))],
        flops=2 * STEPS * 4 * 256 * 256 * width, moved=3_000_000, in_hbm=(3,),
    )
    (parts,) = call(
        block_kernel,
        [((16, 48, 128), BF16)],
        (qpoint_table, home, *far[:2], fit, val, pltpu.with_memory_space_constraint(aside, hbm), screens),
        (smem,) + (vmem,) * 5 + (hbm, vmem),
        [
            pltpu.VMEM((STEPS, 512, 512), BF16), pltpu.VMEM((STEPS, 512, width), BF16),
            pltpu.VMEM((STEPS, 512, width), BF16), pltpu.SemaphoreType.DMA,
        ],
        flops=2 * STEPS * (4 * 256 * 256 + 4 * 4 * 64 * 64) * width,
        moved=3_000_000,
    )
    parts = lax.all_to_all(parts, "ga", 0, 0, axis_index_groups=[GA_ORDER])
    (out,) = call(final_kernel, [((2, STEPS, 8, 128), F32)], (parts,), (vmem,))
    return out[:, :, None]


def solution(mesh):
    in_specs = (P(None, "ka", None, None, None), P(None, None, "ga"), P("ka", None, "ga"), P())
    out_specs = P(None, None, "ka", "ga", None)
    return jax.shard_map(body, mesh=mesh, in_specs=in_specs, out_specs=out_specs, check_vma=False)
```

```python
import jax
import jax.numpy as jnp
from jax import lax
from jax.experimental import pallas as pl
from jax.experimental.pallas import tpu as pltpu
from jax.sharding import PartitionSpec as P

NV = 8
STEPS = 3
GA_ORDER = [8 * half + z for z in (0, 3, 6, 1, 4, 7, 2, 5) for half in range(2)]
KA_ORDER = list(range(15, -1, -1))
BF16 = jnp.bfloat16
F32 = jnp.float32
VMEM_LIMIT = 24 * 1024 * 1024


def call(kernel, out_shapes, operands, spaces, scratch=(), flops=0, moved=0, in_hbm=()):
    specs = [pl.BlockSpec(memory_space=space) for space in spaces]
    out_specs = [
        pl.BlockSpec(memory_space=pltpu.HBM if index in in_hbm else pltpu.VMEM) for index in range(len(out_shapes))
    ]
    return pl.pallas_call(
        kernel,
        out_shape=[
            pltpu.HBM(shape, kind) if index in in_hbm else jax.ShapeDtypeStruct(shape, kind)
            for index, (shape, kind) in enumerate(out_shapes)
        ],
        in_specs=specs,
        out_specs=out_specs,
        scratch_shapes=list(scratch),
        compiler_params=pltpu.CompilerParams(vmem_limit_bytes=VMEM_LIMIT),
        cost_estimate=pl.CostEstimate(flops=flops, bytes_accessed=moved, transcendentals=0),
    )(*operands)


def payload_kernel(screen_ref, out_ref, ready_ref, held_ref, sem):
    copy = pltpu.make_async_copy(screen_ref, held_ref, sem)
    copy.start()
    copy.wait()
    pieces = []
    for q in range(2):
        for j in range(3):
            pieces.append(held_ref[q : q + 1, 256 * j : 256 * (j + 1)])
    rows = jnp.concatenate(pieces + [jnp.zeros((2, 256), F32)], axis=0)
    high = rows.astype(BF16)
    low = (rows - high.astype(F32)).astype(BF16)
    block = jnp.concatenate([high.astype(F32), low.astype(F32)], axis=0).astype(BF16)
    for target in range(16):
        out_ref[target] = block
    ready_ref[...] = block[:, 0:128]


def pair_products(home_ref, far_ref, kind, out_ref):
    for a in range(2):
        top = a * 16 + kind * 8
        home_r = home_ref[top : top + 8, :].astype(F32)[:, None, :]
        home_i = home_ref[32 + top : 40 + top, :].astype(F32)[:, None, :]
        for b in range(2):
            top = b * 16 + kind * 8
            far_r = far_ref[top : top + 8, :].astype(F32)[None]
            far_i = far_ref[32 + top : 40 + top, :].astype(F32)[None]
            real = (home_r * far_r + home_i * far_i).reshape(64, 256).astype(BF16)
            imag = (home_r * far_i - home_i * far_r).reshape(64, 256).astype(BF16)
            at = (a * 2 + b) * 128
            out_ref[at : at + 64, 0:256] = real
            out_ref[at : at + 64, 256:512] = -imag
            out_ref[at + 64 : at + 128, 0:256] = imag
            out_ref[at + 64 : at + 128, 256:512] = real


def density_rows(pair_ref, fit_ref, out_ref):
    for half in range(2):
        at = half * 256
        out_ref[at : at + 256, :] = jnp.dot(
            pair_ref[at : at + 256, :], fit_ref[...], preferred_element_type=F32
        ).astype(BF16)


def pass_kernel(orbital_ref, ready_ref, out_ref):
    out_ref[...] = orbital_ref[...]


def sort_orbitals(crossed_ref, swapped_ref, first_ref, third_ref):
    even = lax.rem(lax.axis_index("ka"), 2) == 0
    crossed, swapped = crossed_ref[...].astype(F32), swapped_ref[...].astype(F32)
    first_ref[...] = jnp.where(even, swapped, crossed).astype(BF16)
    third_ref[...] = jnp.where(even, crossed, swapped).astype(BF16)


def valence_kernel(
    orbital_ref, crossed_ref, far2_ref, swapped_ref, fit_hbm_ref, home_ref, fit_ref, val_ref, aside_ref, far1_ref,
    far3_ref, pair_ref, cond_ref, sems,
):
    home_copy = pltpu.make_async_copy(orbital_ref, home_ref, sems.at[0])
    fit_copy = pltpu.make_async_copy(fit_hbm_ref, fit_ref, sems.at[1])
    home_copy.start()
    fit_copy.start()
    sort_orbitals(crossed_ref, swapped_ref, far1_ref, far3_ref)
    home_copy.wait()
    pair_products(home_ref, far3_ref, 1, pair_ref.at[STEPS])
    for step, far_ref in enumerate((far1_ref, far2_ref, far3_ref)):
        pair_products(home_ref, far_ref, 0, pair_ref.at[step])
    fit_copy.wait()
    density_rows(pair_ref.at[STEPS], fit_ref, cond_ref)
    aside_copy = pltpu.make_async_copy(cond_ref, aside_ref, sems.at[2])
    aside_copy.start()
    for step in range(STEPS):
        density_rows(pair_ref.at[step], fit_ref, val_ref.at[step])
    aside_copy.wait()


def block_kernel(
    table_ref, home_ref, far1_ref, far2_ref, fit_ref, val_ref, aside_ref, screen_ref, out_ref,
    pair_ref, cond_ref, weight_ref, sem,
):
    aside_copy = pltpu.make_async_copy(aside_ref, cond_ref.at[2], sem)
    aside_copy.start()
    first_half = lax.broadcasted_iota(jnp.int32, (64, 128), 1) < 64
    for step, far_ref in enumerate((far1_ref, far2_ref, None)):
        if far_ref is not None:
            pair_products(home_ref, far_ref, 1, pair_ref.at[step])
        rows = screen_ref[KA_ORDER.index(step + 1)].astype(F32)
        rows = rows[0:8] + rows[8:16]
        stored = [
            jnp.concatenate([rows[3 * q + j : 3 * q + j + 1] for j in range(3)], axis=1) for q in range(2)
        ]
        for a in range(2):
            for b in range(2):
                screen = jnp.where(table_ref[a, b] == 0, stored[0], stored[1])
                at = (a * 2 + b) * 128
                weight_ref[step, at : at + 128, :] = (val_ref[step, at : at + 128, :].astype(F32) * screen).astype(BF16)
        if far_ref is not None:
            density_rows(pair_ref.at[step], fit_ref, cond_ref.at[step])
        else:
            aside_copy.wait()
        for a in range(2):
            blocks = []
            for b in range(2):
                at = (a * 2 + b) * 128
                products = lax.dot_general(
                    cond_ref[step, at : at + 128, :], weight_ref[step, at : at + 128, :], (((1,), (1,)), ((), ())),
                    preferred_element_type=F32,
                )
                below = pltpu.roll(products[64:128], 64, 1)
                block = products[0:64] + jnp.where(first_half, below, -below)
                blocks.append(block.reshape(8, 8, 128))
            both = jnp.concatenate(blocks, axis=1).astype(BF16)
            for c in range(8):
                out_ref[GA_ORDER.index(a * 8 + c), step * 16 : (step + 1) * 16, :] = both[c]


def final_kernel(in_ref, out_ref):
    sublane = lax.broadcasted_iota(jnp.int32, (8, 128), 0)
    lane = lax.broadcasted_iota(jnp.int32, (8, 128), 1) // 8
    for step in range(STEPS):
        total = in_ref[0, step * 16 : (step + 1) * 16, :].astype(F32)
        for source in range(1, 16):
            total = total + in_ref[source, step * 16 : (step + 1) * 16, :].astype(F32)
        sides = []
        for b in range(2):
            x = total[b * 8 : (b + 1) * 8]
            for k in range(3):
                bit = 1 << k
                low = (sublane & bit) == 0
                low_lane = (lane & bit) == 0
                from_below = pltpu.roll(pltpu.roll(x, 8 - bit, 0), 8 * bit, 1)
                from_above = pltpu.roll(pltpu.roll(x, bit, 0), 128 - 8 * bit, 1)
                x = jnp.where(low == low_lane, x, jnp.where(low, from_below, from_above))
            sides.append(x)
        first_half = lane < 8
        out_ref[0, step] = jnp.where(first_half, sides[0], pltpu.roll(sides[1], 64, 1))
        out_ref[1, step] = jnp.where(first_half, pltpu.roll(sides[0], 64, 1), sides[1])


def body(orbitals, fit_vectors, screening, qpoint_table):
    vmem, smem = pltpu.VMEM, pltpu.SMEM
    width = fit_vectors.shape[2]

    def shifted(x, by, sources=range(16)):
        return lax.ppermute(x, "ka", [(i, (i + by) % 16) for i in sources])

    hbm = pltpu.HBM
    orbitals = orbitals.reshape(64, 256)
    crossed = lax.ppermute(orbitals, "ka", [(i, (i + (3 if i % 2 else 1)) % 16) for i in range(16)])
    second = shifted(orbitals, 2)
    fit, home, screen = [
        pltpu.with_memory_space_constraint(x, hbm)
        for x in (fit_vectors.reshape(512, width), orbitals, screening[0])
    ]
    payload, ready = call(
        payload_kernel, [((16, 16, 256), BF16), ((16, 128), BF16)], (screen,), (hbm,),
        [pltpu.VMEM((2, width), F32), pltpu.SemaphoreType.DMA], moved=200_000,
    )
    (passed,) = call(
        pass_kernel, [((64, 256), BF16)], (second, ready), (vmem, vmem)
    )
    swapped = lax.ppermute(passed, "ka", [(i, i ^ 1) for i in range(16)])
    far = [crossed, second, swapped]
    screens = lax.all_to_all(payload, "ka", 0, 0, axis_index_groups=[KA_ORDER])
    home, fit, val, aside, first = call(
        valence_kernel,
        [((64, 256), BF16), ((512, width), BF16), ((STEPS, 512, width), BF16), ((512, width), BF16), ((64, 256), BF16)],
        (home, *far, fit), (hbm, vmem, vmem, vmem, hbm),
        [
            pltpu.VMEM((64, 256), BF16), pltpu.VMEM((STEPS + 1, 512, 512), BF16), pltpu.VMEM((512, width), BF16),
            pltpu.SemaphoreType.DMA((3,)),
        ],
        flops=2 * STEPS * 4 * 256 * 256 * width, moved=3_000_000, in_hbm=(3,),
    )
    (parts,) = call(
        block_kernel,
        [((16, 48, 128), BF16)],
        (qpoint_table, home, first, second, fit, val, pltpu.with_memory_space_constraint(aside, hbm), screens),
        (smem,) + (vmem,) * 5 + (hbm, vmem),
        [
            pltpu.VMEM((STEPS, 512, 512), BF16), pltpu.VMEM((STEPS, 512, width), BF16),
            pltpu.VMEM((STEPS, 512, width), BF16), pltpu.SemaphoreType.DMA,
        ],
        flops=2 * STEPS * (4 * 256 * 256 + 4 * 4 * 64 * 64) * width,
        moved=3_000_000,
    )
    parts = lax.all_to_all(parts, "ga", 0, 0, axis_index_groups=[GA_ORDER])
    (out,) = call(final_kernel, [((2, STEPS, 8, 128), F32)], (parts,), (vmem,))
    return out[:, :, None]


def solution(mesh):
    in_specs = (P(None, "ka", None, None, None), P(None, None, "ga"), P("ka", None, "ga"), P())
    out_specs = P(None, None, "ka", "ga", None)
    return jax.shard_map(body, mesh=mesh, in_specs=in_specs, out_specs=out_specs, check_vma=False)
```

```python
import jax
import jax.numpy as jnp
from jax import lax
from jax.experimental import pallas as pl
from jax.experimental.pallas import tpu as pltpu
from jax.sharding import PartitionSpec as P

NV = 8
STEPS = 3
GA_ORDER = list(range(15, -1, -1))
KA_ORDER = list(range(15, -1, -1))
BF16 = jnp.bfloat16
F32 = jnp.float32
VMEM_LIMIT = 24 * 1024 * 1024


def call(kernel, out_shapes, operands, spaces, scratch=(), flops=0, moved=0, in_hbm=()):
    specs = [pl.BlockSpec(memory_space=space) for space in spaces]
    out_specs = [
        pl.BlockSpec(memory_space=pltpu.HBM if index in in_hbm else pltpu.VMEM) for index in range(len(out_shapes))
    ]
    return pl.pallas_call(
        kernel,
        out_shape=[
            pltpu.HBM(shape, kind) if index in in_hbm else jax.ShapeDtypeStruct(shape, kind)
            for index, (shape, kind) in enumerate(out_shapes)
        ],
        in_specs=specs,
        out_specs=out_specs,
        scratch_shapes=list(scratch),
        compiler_params=pltpu.CompilerParams(vmem_limit_bytes=VMEM_LIMIT),
        cost_estimate=pl.CostEstimate(flops=flops, bytes_accessed=moved, transcendentals=0),
    )(*operands)


def payload_kernel(screen_ref, out_ref, held_ref, sem):
    copy = pltpu.make_async_copy(screen_ref, held_ref, sem)
    copy.start()
    copy.wait()
    pieces = []
    for q in range(2):
        for j in range(3):
            pieces.append(held_ref[q : q + 1, 256 * j : 256 * (j + 1)])
    rows = jnp.concatenate(pieces + [jnp.zeros((2, 256), F32)], axis=0)
    high = rows.astype(BF16)
    low = (rows - high.astype(F32)).astype(BF16)
    block = jnp.concatenate([high.astype(F32), low.astype(F32)], axis=0).astype(BF16)
    for target in range(16):
        out_ref[target] = block


def pair_products(home_ref, far_ref, kind, out_ref):
    for a in range(2):
        top = a * 16 + kind * 8
        home_r = home_ref[top : top + 8, :].astype(F32)[:, None, :]
        home_i = home_ref[32 + top : 40 + top, :].astype(F32)[:, None, :]
        for b in range(2):
            top = b * 16 + kind * 8
            far_r = far_ref[top : top + 8, :].astype(F32)[None]
            far_i = far_ref[32 + top : 40 + top, :].astype(F32)[None]
            real = (home_r * far_r + home_i * far_i).reshape(64, 256).astype(BF16)
            imag = (home_r * far_i - home_i * far_r).reshape(64, 256).astype(BF16)
            at = (a * 2 + b) * 128
            out_ref[at : at + 64, 0:256] = real
            out_ref[at : at + 64, 256:512] = -imag
            out_ref[at + 64 : at + 128, 0:256] = imag
            out_ref[at + 64 : at + 128, 256:512] = real


def density_rows(pair_ref, fit_ref, out_ref):
    for half in range(2):
        at = half * 256
        out_ref[at : at + 256, :] = jnp.dot(
            pair_ref[at : at + 256, :], fit_ref[...], preferred_element_type=F32
        ).astype(BF16)


def valence_kernel(
    orbital_ref, far1_ref, far2_ref, far3_ref, fit_hbm_ref, home_ref, fit_ref, val_ref, aside_ref,
    pair_ref, cond_ref, sems,
):
    home_copy = pltpu.make_async_copy(orbital_ref, home_ref, sems.at[0])
    fit_copy = pltpu.make_async_copy(fit_hbm_ref, fit_ref, sems.at[1])
    home_copy.start()
    fit_copy.start()
    home_copy.wait()
    pair_products(home_ref, far3_ref, 1, pair_ref.at[STEPS])
    for step, far_ref in enumerate((far1_ref, far2_ref, far3_ref)):
        pair_products(home_ref, far_ref, 0, pair_ref.at[step])
    fit_copy.wait()
    density_rows(pair_ref.at[STEPS], fit_ref, cond_ref)
    aside_copy = pltpu.make_async_copy(cond_ref, aside_ref, sems.at[2])
    aside_copy.start()
    for step in range(STEPS):
        density_rows(pair_ref.at[step], fit_ref, val_ref.at[step])
    aside_copy.wait()


def block_kernel(
    table_ref, home_ref, far1_ref, far2_ref, fit_ref, val_ref, aside_ref, screen_ref, out_ref,
    pair_ref, cond_ref, weight_ref, sem,
):
    aside_copy = pltpu.make_async_copy(aside_ref, cond_ref.at[2], sem)
    aside_copy.start()
    first_half = lax.broadcasted_iota(jnp.int32, (64, 128), 1) < 64
    for step, far_ref in enumerate((far1_ref, far2_ref, None)):
        if far_ref is not None:
            pair_products(home_ref, far_ref, 1, pair_ref.at[step])
        rows = screen_ref[KA_ORDER.index(step + 1)].astype(F32)
        rows = rows[0:8] + rows[8:16]
        stored = [
            jnp.concatenate([rows[3 * q + j : 3 * q + j + 1] for j in range(3)], axis=1) for q in range(2)
        ]
        for a in range(2):
            for b in range(2):
                screen = jnp.where(table_ref[a, b] == 0, stored[0], stored[1])
                at = (a * 2 + b) * 128
                weight_ref[step, at : at + 128, :] = (val_ref[step, at : at + 128, :].astype(F32) * screen).astype(BF16)
        if far_ref is not None:
            density_rows(pair_ref.at[step], fit_ref, cond_ref.at[step])
        else:
            aside_copy.wait()
        for a in range(2):
            blocks = []
            for b in range(2):
                at = (a * 2 + b) * 128
                products = lax.dot_general(
                    cond_ref[step, at : at + 128, :], weight_ref[step, at : at + 128, :], (((1,), (1,)), ((), ())),
                    preferred_element_type=F32,
                )
                below = pltpu.roll(products[64:128], 64, 1)
                block = products[0:64] + jnp.where(first_half, below, -below)
                blocks.append(block.reshape(8, 8, 128))
            both = jnp.concatenate(blocks, axis=1).astype(BF16)
            for c in range(8):
                out_ref[GA_ORDER.index(a * 8 + c), step * 16 : (step + 1) * 16, :] = both[c]


def final_kernel(in_ref, out_ref):
    sublane = lax.broadcasted_iota(jnp.int32, (8, 128), 0)
    lane = lax.broadcasted_iota(jnp.int32, (8, 128), 1) // 8
    for step in range(STEPS):
        total = in_ref[0, step * 16 : (step + 1) * 16, :].astype(F32)
        for source in range(1, 16):
            total = total + in_ref[source, step * 16 : (step + 1) * 16, :].astype(F32)
        sides = []
        for b in range(2):
            x = total[b * 8 : (b + 1) * 8]
            for k in range(3):
                bit = 1 << k
                low = (sublane & bit) == 0
                low_lane = (lane & bit) == 0
                from_below = pltpu.roll(pltpu.roll(x, 8 - bit, 0), 8 * bit, 1)
                from_above = pltpu.roll(pltpu.roll(x, bit, 0), 128 - 8 * bit, 1)
                x = jnp.where(low == low_lane, x, jnp.where(low, from_below, from_above))
            sides.append(x)
        first_half = lane < 8
        out_ref[0, step] = jnp.where(first_half, sides[0], pltpu.roll(sides[1], 64, 1))
        out_ref[1, step] = jnp.where(first_half, pltpu.roll(sides[0], 64, 1), sides[1])


def body(orbitals, fit_vectors, screening, qpoint_table):
    vmem, smem = pltpu.VMEM, pltpu.SMEM
    width = fit_vectors.shape[2]

    def shifted(x, by, sources=range(16)):
        return lax.ppermute(x, "ka", [(i, (i + by) % 16) for i in sources])

    hbm = pltpu.HBM
    orbitals = orbitals.reshape(64, 256)
    far = [shifted(orbitals, by) for by in range(1, STEPS + 1)]
    fit, home, screen = [
        pltpu.with_memory_space_constraint(x, hbm)
        for x in (fit_vectors.reshape(512, width), orbitals, screening[0])
    ]
    (payload,) = call(
        payload_kernel, [((16, 16, 256), BF16)], (screen,), (hbm,),
        [pltpu.VMEM((2, width), F32), pltpu.SemaphoreType.DMA], moved=200_000,
    )
    screens = lax.all_to_all(payload, "ka", 0, 0, axis_index_groups=[KA_ORDER])
    home, fit, val, aside = call(
        valence_kernel,
        [((64, 256), BF16), ((512, width), BF16), ((STEPS, 512, width), BF16), ((512, width), BF16)],
        (home, *far, fit), (hbm, vmem, vmem, vmem, hbm),
        [pltpu.VMEM((STEPS + 1, 512, 512), BF16), pltpu.VMEM((512, width), BF16), pltpu.SemaphoreType.DMA((3,))],
        flops=2 * STEPS * 4 * 256 * 256 * width, moved=3_000_000, in_hbm=(3,),
    )
    (parts,) = call(
        block_kernel,
        [((16, 48, 128), BF16)],
        (qpoint_table, home, *far[:2], fit, val, pltpu.with_memory_space_constraint(aside, hbm), screens),
        (smem,) + (vmem,) * 5 + (hbm, vmem),
        [
            pltpu.VMEM((STEPS, 512, 512), BF16), pltpu.VMEM((STEPS, 512, width), BF16),
            pltpu.VMEM((STEPS, 512, width), BF16), pltpu.SemaphoreType.DMA,
        ],
        flops=2 * STEPS * (4 * 256 * 256 + 4 * 4 * 64 * 64) * width,
        moved=3_000_000,
    )
    parts = lax.all_to_all(parts, "ga", 0, 0, axis_index_groups=[GA_ORDER])
    (out,) = call(final_kernel, [((2, STEPS, 8, 128), F32)], (parts,), (vmem,))
    return out[:, :, None]


def solution(mesh):
    in_specs = (P(None, "ka", None, None, None), P(None, None, "ga"), P("ka", None, "ga"), P())
    out_specs = P(None, None, "ka", "ga", None)
    return jax.shard_map(body, mesh=mesh, in_specs=in_specs, out_specs=out_specs, check_vma=False)
```

```python
import jax
import jax.numpy as jnp
from jax import lax
from jax.experimental import pallas as pl
from jax.experimental.pallas import tpu as pltpu
from jax.sharding import PartitionSpec as P

NV = 8
STEPS = 3
GA_ORDER = [8 * half + z for z in range(7, -1, -1) for half in (1, 0)]
KA_ORDER = list(range(15, -1, -1))
BF16 = jnp.bfloat16
F32 = jnp.float32
VMEM_LIMIT = 24 * 1024 * 1024


def call(kernel, out_shapes, operands, spaces, scratch=(), flops=0, moved=0, in_hbm=()):
    specs = [pl.BlockSpec(memory_space=space) for space in spaces]
    out_specs = [
        pl.BlockSpec(memory_space=pltpu.HBM if index in in_hbm else pltpu.VMEM) for index in range(len(out_shapes))
    ]
    return pl.pallas_call(
        kernel,
        out_shape=[
            pltpu.HBM(shape, kind) if index in in_hbm else jax.ShapeDtypeStruct(shape, kind)
            for index, (shape, kind) in enumerate(out_shapes)
        ],
        in_specs=specs,
        out_specs=out_specs,
        scratch_shapes=list(scratch),
        compiler_params=pltpu.CompilerParams(vmem_limit_bytes=VMEM_LIMIT),
        cost_estimate=pl.CostEstimate(flops=flops, bytes_accessed=moved, transcendentals=0),
    )(*operands)


def payload_kernel(screen_ref, out_ref, held_ref, sem):
    copy = pltpu.make_async_copy(screen_ref, held_ref, sem)
    copy.start()
    copy.wait()
    pieces = []
    for q in range(2):
        for j in range(3):
            pieces.append(held_ref[q : q + 1, 256 * j : 256 * (j + 1)])
    rows = jnp.concatenate(pieces + [jnp.zeros((2, 256), F32)], axis=0)
    high = rows.astype(BF16)
    low = (rows - high.astype(F32)).astype(BF16)
    block = jnp.concatenate([high.astype(F32), low.astype(F32)], axis=0).astype(BF16)
    for target in range(16):
        out_ref[target] = block


def pair_products(home_ref, far_ref, kind, out_ref):
    for a in range(2):
        top = a * 16 + kind * 8
        home_r = home_ref[top : top + 8, :].astype(F32)[:, None, :]
        home_i = home_ref[32 + top : 40 + top, :].astype(F32)[:, None, :]
        for b in range(2):
            top = b * 16 + kind * 8
            far_r = far_ref[top : top + 8, :].astype(F32)[None]
            far_i = far_ref[32 + top : 40 + top, :].astype(F32)[None]
            real = (home_r * far_r + home_i * far_i).reshape(64, 256).astype(BF16)
            imag = (home_r * far_i - home_i * far_r).reshape(64, 256).astype(BF16)
            at = (a * 2 + b) * 128
            out_ref[at : at + 64, 0:256] = real
            out_ref[at : at + 64, 256:512] = -imag
            out_ref[at + 64 : at + 128, 0:256] = imag
            out_ref[at + 64 : at + 128, 256:512] = real


def density_rows(pair_ref, fit_ref, out_ref):
    for half in range(2):
        at = half * 256
        out_ref[at : at + 256, :] = jnp.dot(
            pair_ref[at : at + 256, :], fit_ref[...], preferred_element_type=F32
        ).astype(BF16)


def valence_kernel(
    orbital_ref, far1_ref, far2_ref, far3_ref, fit_hbm_ref, home_ref, fit_ref, val_ref, aside_ref,
    pair_ref, cond_ref, sems,
):
    home_copy = pltpu.make_async_copy(orbital_ref, home_ref, sems.at[0])
    fit_copy = pltpu.make_async_copy(fit_hbm_ref, fit_ref, sems.at[1])
    home_copy.start()
    fit_copy.start()
    home_copy.wait()
    pair_products(home_ref, far3_ref, 1, pair_ref.at[STEPS])
    for step, far_ref in enumerate((far1_ref, far2_ref, far3_ref)):
        pair_products(home_ref, far_ref, 0, pair_ref.at[step])
    fit_copy.wait()
    density_rows(pair_ref.at[STEPS], fit_ref, cond_ref)
    aside_copy = pltpu.make_async_copy(cond_ref, aside_ref, sems.at[2])
    aside_copy.start()
    for step in range(STEPS):
        density_rows(pair_ref.at[step], fit_ref, val_ref.at[step])
    aside_copy.wait()


def block_kernel(
    table_ref, home_ref, far1_ref, far2_ref, fit_ref, val_ref, aside_ref, screen_ref, out_ref,
    pair_ref, cond_ref, weight_ref, sem,
):
    aside_copy = pltpu.make_async_copy(aside_ref, cond_ref.at[2], sem)
    aside_copy.start()
    first_half = lax.broadcasted_iota(jnp.int32, (64, 128), 1) < 64
    for step, far_ref in enumerate((far1_ref, far2_ref, None)):
        if far_ref is not None:
            pair_products(home_ref, far_ref, 1, pair_ref.at[step])
        rows = screen_ref[KA_ORDER.index(step + 1)].astype(F32)
        rows = rows[0:8] + rows[8:16]
        stored = [
            jnp.concatenate([rows[3 * q + j : 3 * q + j + 1] for j in range(3)], axis=1) for q in range(2)
        ]
        for a in range(2):
            for b in range(2):
                screen = jnp.where(table_ref[a, b] == 0, stored[0], stored[1])
                at = (a * 2 + b) * 128
                weight_ref[step, at : at + 128, :] = (val_ref[step, at : at + 128, :].astype(F32) * screen).astype(BF16)
        if far_ref is not None:
            density_rows(pair_ref.at[step], fit_ref, cond_ref.at[step])
        else:
            aside_copy.wait()
        for a in range(2):
            blocks = []
            for b in range(2):
                at = (a * 2 + b) * 128
                products = lax.dot_general(
                    cond_ref[step, at : at + 128, :], weight_ref[step, at : at + 128, :], (((1,), (1,)), ((), ())),
                    preferred_element_type=F32,
                )
                below = pltpu.roll(products[64:128], 64, 1)
                block = products[0:64] + jnp.where(first_half, below, -below)
                blocks.append(block.reshape(8, 8, 128))
            both = jnp.concatenate(blocks, axis=1).astype(BF16)
            for c in range(8):
                out_ref[GA_ORDER.index(a * 8 + c), step * 16 : (step + 1) * 16, :] = both[c]


def final_kernel(in_ref, out_ref):
    sublane = lax.broadcasted_iota(jnp.int32, (8, 128), 0)
    lane = lax.broadcasted_iota(jnp.int32, (8, 128), 1) // 8
    for step in range(STEPS):
        total = in_ref[0, step * 16 : (step + 1) * 16, :].astype(F32)
        for source in range(1, 16):
            total = total + in_ref[source, step * 16 : (step + 1) * 16, :].astype(F32)
        sides = []
        for b in range(2):
            x = total[b * 8 : (b + 1) * 8]
            for k in range(3):
                bit = 1 << k
                low = (sublane & bit) == 0
                low_lane = (lane & bit) == 0
                from_below = pltpu.roll(pltpu.roll(x, 8 - bit, 0), 8 * bit, 1)
                from_above = pltpu.roll(pltpu.roll(x, bit, 0), 128 - 8 * bit, 1)
                x = jnp.where(low == low_lane, x, jnp.where(low, from_below, from_above))
            sides.append(x)
        first_half = lane < 8
        out_ref[0, step] = jnp.where(first_half, sides[0], pltpu.roll(sides[1], 64, 1))
        out_ref[1, step] = jnp.where(first_half, pltpu.roll(sides[0], 64, 1), sides[1])


def body(orbitals, fit_vectors, screening, qpoint_table):
    vmem, smem = pltpu.VMEM, pltpu.SMEM
    width = fit_vectors.shape[2]

    def shifted(x, by, sources=range(16)):
        return lax.ppermute(x, "ka", [(i, (i + by) % 16) for i in sources])

    hbm = pltpu.HBM
    orbitals = orbitals.reshape(64, 256)
    far = [shifted(orbitals, by) for by in range(1, STEPS + 1)]
    fit, home, screen = [
        pltpu.with_memory_space_constraint(x, hbm)
        for x in (fit_vectors.reshape(512, width), orbitals, screening[0])
    ]
    (payload,) = call(
        payload_kernel, [((16, 16, 256), BF16)], (screen,), (hbm,),
        [pltpu.VMEM((2, width), F32), pltpu.SemaphoreType.DMA], moved=200_000,
    )
    screens = lax.all_to_all(payload, "ka", 0, 0, axis_index_groups=[KA_ORDER])
    home, fit, val, aside = call(
        valence_kernel,
        [((64, 256), BF16), ((512, width), BF16), ((STEPS, 512, width), BF16), ((512, width), BF16)],
        (home, *far, fit), (hbm, vmem, vmem, vmem, hbm),
        [pltpu.VMEM((STEPS + 1, 512, 512), BF16), pltpu.VMEM((512, width), BF16), pltpu.SemaphoreType.DMA((3,))],
        flops=2 * STEPS * 4 * 256 * 256 * width, moved=3_000_000, in_hbm=(3,),
    )
    (parts,) = call(
        block_kernel,
        [((16, 48, 128), BF16)],
        (qpoint_table, home, *far[:2], fit, val, pltpu.with_memory_space_constraint(aside, hbm), screens),
        (smem,) + (vmem,) * 5 + (hbm, vmem),
        [
            pltpu.VMEM((STEPS, 512, 512), BF16), pltpu.VMEM((STEPS, 512, width), BF16),
            pltpu.VMEM((STEPS, 512, width), BF16), pltpu.SemaphoreType.DMA,
        ],
        flops=2 * STEPS * (4 * 256 * 256 + 4 * 4 * 64 * 64) * width,
        moved=3_000_000,
    )
    parts = lax.all_to_all(parts, "ga", 0, 0, axis_index_groups=[GA_ORDER])
    (out,) = call(final_kernel, [((2, STEPS, 8, 128), F32)], (parts,), (vmem,))
    return out[:, :, None]


def solution(mesh):
    in_specs = (P(None, "ka", None, None, None), P(None, None, "ga"), P("ka", None, "ga"), P())
    out_specs = P(None, None, "ka", "ga", None)
    return jax.shard_map(body, mesh=mesh, in_specs=in_specs, out_specs=out_specs, check_vma=False)
```

```python
import jax
import jax.numpy as jnp
from jax import lax
from jax.experimental import pallas as pl
from jax.experimental.pallas import tpu as pltpu
from jax.sharding import PartitionSpec as P

NV = 8
STEPS = 3
GA_ORDER = [8 * half + z for z in (7, 3, 6, 2, 5, 1, 4, 0) for half in (1, 0)]
KA_ORDER = list(range(15, -1, -1))
BF16 = jnp.bfloat16
F32 = jnp.float32
VMEM_LIMIT = 24 * 1024 * 1024


def call(kernel, out_shapes, operands, spaces, scratch=(), flops=0, moved=0, in_hbm=()):
    specs = [pl.BlockSpec(memory_space=space) for space in spaces]
    out_specs = [
        pl.BlockSpec(memory_space=pltpu.HBM if index in in_hbm else pltpu.VMEM) for index in range(len(out_shapes))
    ]
    return pl.pallas_call(
        kernel,
        out_shape=[
            pltpu.HBM(shape, kind) if index in in_hbm else jax.ShapeDtypeStruct(shape, kind)
            for index, (shape, kind) in enumerate(out_shapes)
        ],
        in_specs=specs,
        out_specs=out_specs,
        scratch_shapes=list(scratch),
        compiler_params=pltpu.CompilerParams(vmem_limit_bytes=VMEM_LIMIT),
        cost_estimate=pl.CostEstimate(flops=flops, bytes_accessed=moved, transcendentals=0),
    )(*operands)


def payload_kernel(screen_ref, out_ref, held_ref, sem):
    copy = pltpu.make_async_copy(screen_ref, held_ref, sem)
    copy.start()
    copy.wait()
    pieces = []
    for q in range(2):
        for j in range(3):
            pieces.append(held_ref[q : q + 1, 256 * j : 256 * (j + 1)])
    rows = jnp.concatenate(pieces + [jnp.zeros((2, 256), F32)], axis=0)
    high = rows.astype(BF16)
    low = (rows - high.astype(F32)).astype(BF16)
    block = jnp.concatenate([high.astype(F32), low.astype(F32)], axis=0).astype(BF16)
    for target in range(16):
        out_ref[target] = block


def pair_products(home_ref, far_ref, kind, out_ref):
    for a in range(2):
        top = a * 16 + kind * 8
        home_r = home_ref[top : top + 8, :].astype(F32)[:, None, :]
        home_i = home_ref[32 + top : 40 + top, :].astype(F32)[:, None, :]
        for b in range(2):
            top = b * 16 + kind * 8
            far_r = far_ref[top : top + 8, :].astype(F32)[None]
            far_i = far_ref[32 + top : 40 + top, :].astype(F32)[None]
            real = (home_r * far_r + home_i * far_i).reshape(64, 256).astype(BF16)
            imag = (home_r * far_i - home_i * far_r).reshape(64, 256).astype(BF16)
            at = (a * 2 + b) * 128
            out_ref[at : at + 64, 0:256] = real
            out_ref[at : at + 64, 256:512] = -imag
            out_ref[at + 64 : at + 128, 0:256] = imag
            out_ref[at + 64 : at + 128, 256:512] = real


def density_rows(pair_ref, fit_ref, out_ref):
    for half in range(2):
        at = half * 256
        out_ref[at : at + 256, :] = jnp.dot(
            pair_ref[at : at + 256, :], fit_ref[...], preferred_element_type=F32
        ).astype(BF16)


def valence_kernel(
    orbital_ref, far1_ref, far2_ref, far3_ref, fit_hbm_ref, home_ref, fit_ref, val_ref, aside_ref,
    pair_ref, cond_ref, sems,
):
    home_copy = pltpu.make_async_copy(orbital_ref, home_ref, sems.at[0])
    fit_copy = pltpu.make_async_copy(fit_hbm_ref, fit_ref, sems.at[1])
    home_copy.start()
    fit_copy.start()
    home_copy.wait()
    pair_products(home_ref, far3_ref, 1, pair_ref.at[STEPS])
    for step, far_ref in enumerate((far1_ref, far2_ref, far3_ref)):
        pair_products(home_ref, far_ref, 0, pair_ref.at[step])
    fit_copy.wait()
    density_rows(pair_ref.at[STEPS], fit_ref, cond_ref)
    aside_copy = pltpu.make_async_copy(cond_ref, aside_ref, sems.at[2])
    aside_copy.start()
    for step in range(STEPS):
        density_rows(pair_ref.at[step], fit_ref, val_ref.at[step])
    aside_copy.wait()


def block_kernel(
    table_ref, home_ref, far1_ref, far2_ref, fit_ref, val_ref, aside_ref, screen_ref, out_ref,
    pair_ref, cond_ref, weight_ref, sem,
):
    aside_copy = pltpu.make_async_copy(aside_ref, cond_ref.at[2], sem)
    aside_copy.start()
    first_half = lax.broadcasted_iota(jnp.int32, (64, 128), 1) < 64
    for step, far_ref in enumerate((far1_ref, far2_ref, None)):
        if far_ref is not None:
            pair_products(home_ref, far_ref, 1, pair_ref.at[step])
        rows = screen_ref[KA_ORDER.index(step + 1)].astype(F32)
        rows = rows[0:8] + rows[8:16]
        stored = [
            jnp.concatenate([rows[3 * q + j : 3 * q + j + 1] for j in range(3)], axis=1) for q in range(2)
        ]
        for a in range(2):
            for b in range(2):
                screen = jnp.where(table_ref[a, b] == 0, stored[0], stored[1])
                at = (a * 2 + b) * 128
                weight_ref[step, at : at + 128, :] = (val_ref[step, at : at + 128, :].astype(F32) * screen).astype(BF16)
        if far_ref is not None:
            density_rows(pair_ref.at[step], fit_ref, cond_ref.at[step])
        else:
            aside_copy.wait()
        for a in range(2):
            blocks = []
            for b in range(2):
                at = (a * 2 + b) * 128
                products = lax.dot_general(
                    cond_ref[step, at : at + 128, :], weight_ref[step, at : at + 128, :], (((1,), (1,)), ((), ())),
                    preferred_element_type=F32,
                )
                below = pltpu.roll(products[64:128], 64, 1)
                block = products[0:64] + jnp.where(first_half, below, -below)
                blocks.append(block.reshape(8, 8, 128))
            both = jnp.concatenate(blocks, axis=1).astype(BF16)
            for c in range(8):
                out_ref[GA_ORDER.index(a * 8 + c), step * 16 : (step + 1) * 16, :] = both[c]


def final_kernel(in_ref, out_ref):
    sublane = lax.broadcasted_iota(jnp.int32, (8, 128), 0)
    lane = lax.broadcasted_iota(jnp.int32, (8, 128), 1) // 8
    for step in range(STEPS):
        total = in_ref[0, step * 16 : (step + 1) * 16, :].astype(F32)
        for source in range(1, 16):
            total = total + in_ref[source, step * 16 : (step + 1) * 16, :].astype(F32)
        sides = []
        for b in range(2):
            x = total[b * 8 : (b + 1) * 8]
            for k in range(3):
                bit = 1 << k
                low = (sublane & bit) == 0
                low_lane = (lane & bit) == 0
                from_below = pltpu.roll(pltpu.roll(x, 8 - bit, 0), 8 * bit, 1)
                from_above = pltpu.roll(pltpu.roll(x, bit, 0), 128 - 8 * bit, 1)
                x = jnp.where(low == low_lane, x, jnp.where(low, from_below, from_above))
            sides.append(x)
        first_half = lane < 8
        out_ref[0, step] = jnp.where(first_half, sides[0], pltpu.roll(sides[1], 64, 1))
        out_ref[1, step] = jnp.where(first_half, pltpu.roll(sides[0], 64, 1), sides[1])


def body(orbitals, fit_vectors, screening, qpoint_table):
    vmem, smem = pltpu.VMEM, pltpu.SMEM
    width = fit_vectors.shape[2]

    def shifted(x, by, sources=range(16)):
        return lax.ppermute(x, "ka", [(i, (i + by) % 16) for i in sources])

    hbm = pltpu.HBM
    orbitals = orbitals.reshape(64, 256)
    far = [shifted(orbitals, by) for by in range(1, STEPS + 1)]
    fit, home, screen = [
        pltpu.with_memory_space_constraint(x, hbm)
        for x in (fit_vectors.reshape(512, width), orbitals, screening[0])
    ]
    (payload,) = call(
        payload_kernel, [((16, 16, 256), BF16)], (screen,), (hbm,),
        [pltpu.VMEM((2, width), F32), pltpu.SemaphoreType.DMA], moved=200_000,
    )
    screens = lax.all_to_all(payload, "ka", 0, 0, axis_index_groups=[KA_ORDER])
    home, fit, val, aside = call(
        valence_kernel,
        [((64, 256), BF16), ((512, width), BF16), ((STEPS, 512, width), BF16), ((512, width), BF16)],
        (home, *far, fit), (hbm, vmem, vmem, vmem, hbm),
        [pltpu.VMEM((STEPS + 1, 512, 512), BF16), pltpu.VMEM((512, width), BF16), pltpu.SemaphoreType.DMA((3,))],
        flops=2 * STEPS * 4 * 256 * 256 * width, moved=3_000_000, in_hbm=(3,),
    )
    (parts,) = call(
        block_kernel,
        [((16, 48, 128), BF16)],
        (qpoint_table, home, *far[:2], fit, val, pltpu.with_memory_space_constraint(aside, hbm), screens),
        (smem,) + (vmem,) * 5 + (hbm, vmem),
        [
            pltpu.VMEM((STEPS, 512, 512), BF16), pltpu.VMEM((STEPS, 512, width), BF16),
            pltpu.VMEM((STEPS, 512, width), BF16), pltpu.SemaphoreType.DMA,
        ],
        flops=2 * STEPS * (4 * 256 * 256 + 4 * 4 * 64 * 64) * width,
        moved=3_000_000,
    )
    parts = lax.all_to_all(parts, "ga", 0, 0, axis_index_groups=[GA_ORDER])
    (out,) = call(final_kernel, [((2, STEPS, 8, 128), F32)], (parts,), (vmem,))
    return out[:, :, None]


def solution(mesh):
    in_specs = (P(None, "ka", None, None, None), P(None, None, "ga"), P("ka", None, "ga"), P())
    out_specs = P(None, None, "ka", "ga", None)
    return jax.shard_map(body, mesh=mesh, in_specs=in_specs, out_specs=out_specs, check_vma=False)
```
